32 devices in a mesh: dp: 8 (over y, x, core), mp: 4 (over z).
Axes of the slice: x: 2, y: 2, z: 4, core: 2. Of those that a mesh axis runs over, the one named last changes fastest.
Arguments:
- block_in: bfloat16 [8192, 1536], P(('dp', 'mp')), may hold values from -6 to 6
- grad_out: bfloat16 [8192, 1536], P(('dp', 'mp')), may hold values from -6 to 6
- resets: int32 [8, 16], P('dp'), may hold values 0 or 1
- counts: int32 [8], P('dp'), may hold values from 512 to 1024
- gain_in: bfloat16 [1536], P(('dp', 'mp')), may hold values from 0.5 to 1.5
- w_forget: bfloat16 [1536], P(('dp', 'mp')), may hold values from -2.5 to 2.5
- w_momentum: bfloat16 [1536], P(('dp', 'mp')), may hold values from -2.5 to 2.5
- project_in: bfloat16 [3, 1536, 1536], P(None, 'dp', 'mp'), may hold values from -0.15625 to 0.15625
- project_out: bfloat16 [1536, 1536], P('mp', 'dp'), may hold values from -0.625 to 0.625
- memory_in: bfloat16 [1536, 6144], P('dp', 'mp'), may hold values from -0.15625 to 0.15625
- memory_out: bfloat16 [6144, 1536], P('mp', 'dp'), may hold values from -0.078125 to 0.078125
- gain_mid: bfloat16 [1536], P(('dp', 'mp')), may hold values from 0.5 to 1.5
- gate_weight: bfloat16 [1536, 4096], P('dp', 'mp'), may hold values from -0.15625 to 0.15625
- up_weight: bfloat16 [1536, 4096], P('dp', 'mp'), may hold values from -0.15625 to 0.15625
- down_weight: bfloat16 [4096, 1536], P('mp', 'dp'), may hold values from -0.09375 to 0.09375
Outputs:
- block_out: bfloat16 [8192, 1536], P(('dp', 'mp'))
- grad_block_in: float32 [8192, 1536], P(('dp', 'mp'))
- grad_gain_in: float32 [1536], P(('dp', 'mp'))
- grad_forget: float32 [1536], P(('dp', 'mp'))
- grad_momentum: float32 [1536], P(('dp', 'mp'))
- grad_project_in: float32 [3, 1536, 1536], P(None, 'dp', 'mp')
- grad_project_out: float32 [1536, 1536], P('mp', 'dp')
- grad_memory_in: float32 [1536, 6144], P('dp', 'mp')
- grad_memory_out: float32 [6144, 1536], P('mp', 'dp')
- grad_gain_mid: float32 [1536], P(('dp', 'mp'))
- grad_gate: float32 [1536, 4096], P('dp', 'mp')
- grad_up: float32 [1536, 4096], P('dp', 'mp')
- grad_down: float32 [4096, 1536], P('mp', 'dp')
- logged: float32 [3], replicated
The draws below stay inside these ranges and needn't reach their ends.
All inputs are finite; a program needn't handle non-finite values. No bound on the sum of `resets` on one device may be relied on, other than what follows from the above.
Results may differ from the reference program's by a relative error of at most 0.01.
Values may be sent and summed in bfloat16 or wider, within the bound.
A program may use at most 256 MiB of HBM per device.

```python
import jax
import jax.numpy as jnp
from jax import lax

D = 1536
NH = 16
HD = 96
FF = 4096
HM = 6144
CH = 64
SEQ = 1024
ROWS = 8
SPANS = 16
TOKENS = 8192


def place_ends(array, stream_key, smallest, high):
    place = [jax.random.randint(jax.random.fold_in(stream_key, axis), (), 0, length) for axis, length in enumerate(array.shape)]
    main_axis = array.shape.index(max(array.shape))
    next_to = place[:main_axis] + [(place[main_axis] + 1) % array.shape[main_axis]] + place[main_axis + 1:]
    return array.at[tuple(place)].set(smallest).at[tuple(next_to)].set(high)


def level_of(key, extent, pieces, smallest, top_value):
    factor_of, own = 1.0, jax.random.fold_in(key, 6)
    for position, parts in pieces:
        heights = jnp.exp(jax.random.uniform(jax.random.fold_in(own, position), (parts,), jnp.float32, smallest / len(pieces), top_value / len(pieces)))
        factor_of = factor_of * jnp.repeat(heights, extent[position] // parts).reshape([-1 if axis == position else 1 for axis in range(len(extent))])
    return factor_of


def centred(key, dims, scale, bound, pieces=(), kind=jnp.bfloat16):
    values = jax.random.normal(key, dims, jnp.float32) * scale
    if len(pieces) > 0:
        values = level_of(key, dims, pieces, -0.22, 0.18) * values
    return jnp.clip(values, min=-bound, max=bound).astype(kind)


def setup_inputs(seed: int = 0) -> dict:
    streams_of = jax.random.split(jax.random.key(seed), 16)
    block_in = centred(streams_of[0], (TOKENS, D), 1.0, 6.0, ((0, 32),))
    grad_out = centred(streams_of[1], (TOKENS, D), 1.0, 6.0, ((0, 32),))
    resets = place_ends((jax.random.randint(streams_of[2], (ROWS, SPANS), 0, 4) < 1).astype(jnp.int32), jax.random.fold_in(streams_of[2], 1), 0, 1)
    counts = place_ends(jax.random.randint(streams_of[3], (ROWS,), SEQ // 2, SEQ + 1), jax.random.fold_in(streams_of[3], 1), SEQ // 2, SEQ).astype(jnp.int32)
    gain_in = jnp.clip(1.0 + 0.1 * jax.random.normal(streams_of[4], (D,), jnp.float32), 0.5, 1.5).astype(jnp.bfloat16)
    w_forget = centred(streams_of[5], (D,), (max(D // 256, 1)) ** -0.5, 2.5, ((0, 32),))
    w_momentum = centred(streams_of[6], (D,), (max(D // 256, 1)) ** -0.5, 2.5, ((0, 32),))
    project_in = centred(streams_of[7], (3, D, NH * HD), D ** -0.5, 0.15625, ((1, 8), (2, 4)))
    project_out = centred(streams_of[8], (NH * HD, D), (NH * HD // 16) ** -0.5, 0.625, ((0, 4), (1, 8)))
    memory_in = centred(streams_of[9], (D, HM), D ** -0.5, 0.15625, ((0, 8), (1, 4)))
    memory_out = centred(streams_of[10], (HM, D), HM ** -0.5, 0.078125, ((0, 4), (1, 8)))
    gain_mid = jnp.clip(1.0 + 0.1 * jax.random.normal(streams_of[11], (D,), jnp.float32), 0.5, 1.5).astype(jnp.bfloat16)
    gate_weight = centred(streams_of[12], (D, FF), D ** -0.5, 0.15625, ((0, 8), (1, 4)))
    up_weight = centred(streams_of[13], (D, FF), D ** -0.5, 0.15625, ((0, 8), (1, 4)))
    down_weight = centred(streams_of[14], (FF, D), FF ** -0.5, 0.09375, ((0, 4), (1, 8)))
    return dict(block_in=block_in, grad_out=grad_out, resets=resets, counts=counts, gain_in=gain_in, w_forget=w_forget, w_momentum=w_momentum, project_in=project_in, project_out=project_out, memory_in=memory_in, memory_out=memory_out, gain_mid=gain_mid, gate_weight=gate_weight, up_weight=up_weight, down_weight=down_weight)


EPS = 1e-06
ALPHA_SHIFT = 1.5
ETA_SHIFT = 0.5
NEG = -1e+30

@jax.custom_vjp
def low(v):
    return lax.optimization_barrier(v.astype(jnp.bfloat16)).astype(jnp.float32)

@jax.custom_vjp
def low_back(v):
    return v

def low_keep(v):
    return (low(v), None)

def low_pass(kept, grad):
    return (grad,)

def back_keep(v):
    return (v, None)

def back_low(kept, grad):
    return (low(grad),)
low.defvjp(low_keep, low_pass)
low_back.defvjp(back_keep, back_low)

def norm_rows(values, gain):
    return values * lax.rsqrt(lax.optimization_barrier(jnp.mean(values * values, axis=-1, keepdims=True)) + EPS) * gain

def span_weights(alpha, eta, keep):
    number = alpha.shape[0]
    basis = jnp.eye(number, dtype=alpha.dtype)

    def advance(carry, inputs):
        state, memory = carry
        rate, moment, kept, unit = inputs
        before = memory * kept
        state = moment * kept * state + unit
        memory = rate * kept * memory + state
        return ((state, memory), before)
    start = (jnp.zeros(number, alpha.dtype), jnp.zeros(number, alpha.dtype))
    _, table = lax.scan(advance, start, (alpha, eta, keep, basis))
    return table

def row_forward(row_in, params, reset_row, count):
    gain_one, forget_vec, moment_vec, project_in, project_out, memory_in, memory_out, gain_two, gate_weight, up_weight, down_weight = params
    high = lax.Precision.HIGHEST
    length = row_in.shape[0]
    spans = length // CH
    positions = jnp.arange(length, dtype=jnp.int32)
    valid = (positions < count).astype(jnp.float32)
    keep = (1 - reset_row).astype(jnp.float32)
    doc_tok = jnp.repeat(jnp.cumsum(reset_row, dtype=jnp.int32), CH)
    normed = low(norm_rows(row_in, gain_one))
    logits = jnp.dot(normed, jnp.stack([forget_vec, moment_vec], axis=1), precision=high)
    logits = lax.optimization_barrier(jnp.mean(logits.reshape(spans, CH, 2), axis=1))
    alpha = jax.nn.sigmoid(logits[:, 0] + ALPHA_SHIFT)
    eta = jax.nn.sigmoid(logits[:, 1] + ETA_SHIFT)
    table = span_weights(alpha, eta, keep)
    spread = jnp.repeat(jnp.repeat(table, CH, axis=0), CH, axis=1)
    pre_act = low_back(jnp.dot(normed, memory_in, precision=high))
    features = low(jax.nn.silu(pre_act))
    sim = low_back(jnp.dot(features, features.T, precision=high) / HM)
    mixing = low(sim * spread * valid[None, :] / CH)
    recall = jnp.dot(features, memory_out, precision=high) + jnp.dot(mixing, normed, precision=high)
    triple = low(low_back(jnp.einsum('td,kde->kte', normed, project_in, precision=high)))
    query = triple[0].reshape(length, NH, HD)
    keys = triple[1].reshape(length, NH, HD)
    values = triple[2].reshape(length, NH, HD)
    block = min(512, length)
    scale = HD ** (-0.5)

    def attend(start):
        rows = start + jnp.arange(block, dtype=jnp.int32)
        query_rows = lax.dynamic_slice_in_dim(query, start, block, 0)
        doc_rows = lax.dynamic_slice_in_dim(doc_tok, start, block, 0)
        score = low_back(jnp.einsum('thd,shd->hts', query_rows, keys, precision=high) * scale)
        allow = (positions[None, :] <= rows[:, None]) & (doc_tok[None, :] == doc_rows[:, None]) & ((valid[None, :] > 0) | (positions[None, :] == rows[:, None]))
        score = jnp.where(allow[None], score, NEG)
        prob = jax.nn.softmax(score, axis=-1)
        return jnp.einsum('hts,shd->thd', low(prob), values, precision=high)
    starts = jnp.arange(length // block, dtype=jnp.int32) * block
    context = lax.map(jax.checkpoint(attend), starts).reshape(length, NH * HD)
    context = low(low_back(context))
    branch = low_back(recall + jnp.dot(context, project_out, precision=high))
    middle = row_in + branch
    normed_two = low(norm_rows(middle, gain_two))
    gate_pre = low_back(jnp.dot(normed_two, gate_weight, precision=high))
    up_pre = low_back(jnp.dot(normed_two, up_weight, precision=high))
    hidden = low(jax.nn.silu(gate_pre) * up_pre)
    result = middle + low_back(jnp.dot(hidden, down_weight, precision=high))
    feature_blocks = features.reshape(spans, CH, HM)
    gram = jnp.einsum('cth,csh->cts', feature_blocks, feature_blocks, precision=high)
    written = (normed * valid[:, None]).reshape(spans, CH, D)
    cross = jnp.einsum('ctd,csd->cts', written, written, precision=high)
    piece = lax.optimization_barrier(jnp.sum(gram * cross, axis=(1, 2)))
    surprise = jnp.sqrt(piece / (HM * D * CH))
    weight = lax.optimization_barrier(jnp.sum(valid.reshape(spans, CH), axis=1))
    numer = jnp.stack([jnp.sum(weight * surprise), jnp.sum(weight * alpha), jnp.sum(weight * eta)])
    return (result, (numer, jnp.sum(weight)))

def reference(block_in, grad_out, resets, counts, gain_in, w_forget, w_momentum, project_in, project_out, memory_in, memory_out, gain_mid, gate_weight, up_weight, down_weight):
    params = tuple((p.astype(jnp.float32) for p in (gain_in, w_forget, w_momentum, project_in, project_out, memory_in, memory_out, gain_mid, gate_weight, up_weight, down_weight)))
    rows_in = block_in.astype(jnp.float32).reshape(ROWS, SEQ, D)
    rows_grad = grad_out.astype(jnp.float32).reshape(ROWS, SEQ, D)

    def one_row(total, inputs):
        row_in, row_grad, reset_row, count = inputs

        def forward(values, weights):
            return row_forward(values, weights, reset_row, count)
        result, pull, extras = jax.vjp(forward, row_in, params, has_aux=True)
        grad_row, grad_params = pull(row_grad)
        total = jax.tree.map(lambda a, b: a + b, total, grad_params)
        return (total, (result, grad_row, extras[0], extras[1]))
    zero = jax.tree.map(jnp.zeros_like, params)
    grads, (results, grad_rows, numers, weights) = lax.scan(one_row, zero, (rows_in, rows_grad, resets, counts))
    logged = lax.optimization_barrier(jnp.sum(numers, axis=0)) / jnp.sum(weights)
    return (results.reshape(TOKENS, D).astype(jnp.bfloat16), grad_rows.reshape(TOKENS, D), grads[0], grads[1], grads[2], grads[3], grads[4], grads[5], grads[6], grads[7], grads[8], grads[9], grads[10], logged)
```

```python
import functools

import jax
import jax.numpy as jnp
from jax import lax
from jax.experimental import pallas as pl
from jax.experimental.pallas import tpu as pltpu
from jax.sharding import Mesh
from jax.sharding import PartitionSpec as P

HD = 96
CH = 64
EPS = 1e-06
ALPHA_SHIFT = 1.5
ETA_SHIFT = 0.5
NEG = -1e30
SCALE = HD ** (-0.5)
F32 = jnp.float32
BF16 = jnp.bfloat16
VMEM_LIMIT = 24 * 1024 * 1024

def dot(a, b, ca, cb):
    return lax.dot_general(a, b, (((ca,), (cb,)), ((), ())), preferred_element_type=F32)


def swap(x, axis):
    return lax.ppermute(x, axis, [(0, 1), (1, 0)])


def turn(x):
    return lax.ppermute(x, ("c", "h"), [(0, 0), (1, 2), (2, 1), (3, 3)])


def after(x, *others):
    return lax.optimization_barrier((x,) + others)[0]


def cat(parts, axis=0):
    return jnp.concatenate(parts, axis=axis)


def by_index(index, first, second, axis=0):
    return jnp.where(index == 0, cat([first, second], axis), cat([second, first], axis))


def gather_rows(x):
    c, l = lax.axis_index("c"), lax.axis_index("l")
    half = by_index(l, x, swap(x, "l"))
    return by_index(c, half, swap(half, "c"))


def scatter_rows(x):
    c, l = lax.axis_index("c"), lax.axis_index("l")
    rows = x.shape[0] // 2
    send = lax.dynamic_slice_in_dim(x, (1 - c) * rows, rows, 0).astype(BF16)
    half = lax.dynamic_slice_in_dim(x, c * rows, rows, 0).astype(F32) + swap(send, "c").astype(F32)
    rows = rows // 2
    send = lax.dynamic_slice_in_dim(half, (1 - l) * rows, rows, 0).astype(BF16)
    return lax.dynamic_slice_in_dim(half, l * rows, rows, 0) + swap(send, "l").astype(F32)


def shuffle(plane, v, back=False):
    if len(plane) == 1:
        return v
    share = v.shape[-1] // 4
    b = [v[..., i * share : (i + 1) * share] for i in range(4)]
    if back:
        b = [b[0], b[1], b[3], b[2]]
    x, y = lax.axis_index("x"), lax.axis_index("y")
    b = [jnp.where(x == 0, b[i], b[i ^ 1]) for i in range(4)]
    b = [jnp.where(y == 0, b[i], b[i ^ 2]) for i in range(4)]
    if not back:
        b = [b[0], b[1], b[3], b[2]]
    return cat(b, -1)


def gather_plane(plane, piece, first):
    if len(plane) == 1:
        whole = lax.all_gather(piece, plane, axis=0, tiled=True)
        return whole, piece
    near = {axis: swap(piece, axis) for axis in plane}
    second = "y" if first == "x" else "x"
    far = swap(near[first], second)
    return cat([piece, near["x"], far, near["y"]]), near[first]


def scatter_plane(plane, pairs, first, wait):
    def product(start, stop):
        parts = [dot(left[:, start:stop], right, 0, 0).astype(BF16) for left, right in pairs]
        return cat(parts, 1) if len(parts) > 1 else parts[0]

    width = pairs[0][0].shape[1]
    if len(plane) == 1:
        whole = product(0, width)
        return lax.psum_scatter(whole, plane, scatter_dimension=0, tiled=True).astype(F32)
    w = width // 4
    if first == "x":
        got = swap(wait(product(w, 3 * w)), "x")
        second, mine, other, other_at = "y", got[:w], got[w:], 3
    else:
        got = swap(wait(product(2 * w, 4 * w)), "y")
        second, mine, other, other_at = "x", got[w:], got[:w], 1
    other = product(other_at * w, (other_at + 1) * w).astype(F32) + other.astype(F32)
    other = swap(other.astype(BF16), second)
    mine = product(0, w).astype(F32) + mine.astype(F32)
    return mine + other.astype(F32)


def reduce_group(plane, sources, wait=lambda v: v):
    here = scatter_plane(plane, [(left, right) for left, right, _ in sources], "x", wait)
    there = scatter_plane(plane, [(left, right) for left, _, right in sources], "y", wait)
    mine = here + swap(there.astype(BF16), "h").astype(F32)
    c = lax.axis_index("c")
    rows = mine.shape[0] // 2
    given = lax.dynamic_slice_in_dim(mine, (1 - c) * rows, rows, 0).astype(BF16)
    kept = lax.dynamic_slice_in_dim(mine, c * rows, rows, 0)
    got = swap(given, "c").astype(F32)
    results, start = [], 0
    for _, right, _ in sources:
        n = right.shape[1]
        results.append(by_index(c, kept[:, start : start + n], got[:, start : start + n], 1))
        start += n
    return results


def pack(shards):
    c = lax.axis_index("c")
    low = cat([s[:, : s.shape[1] // 2] for s in shards], 1)
    high = cat([s[:, s.shape[1] // 2 :] for s in shards], 1)
    mine = jnp.where(c == 0, low, high)
    got = swap(jnp.where(c == 0, high, low), "c")
    return by_index(c, mine, got)


def tall(x):
    padding = 128 - x.shape[0]
    wide = cat([x.astype(F32), jnp.zeros((padding, x.shape[1]), F32)])
    return wide.astype(BF16), wide.T.astype(BF16)


def attend_kernel(code_ref, doc_ref, qkv_ref, ctx_ref, lse_ref, bias_ref):
    length = qkv_ref.shape[-1]
    heads = qkv_ref.shape[0] // (3 * HD)
    block = min(256, length)
    fill_bias(code_ref, doc_ref, bias_ref)
    for head in range(heads):
        part = [slice((i * heads + head) * HD, (i * heads + head + 1) * HD) for i in range(3)]
        v = qkv_ref[part[2]]
        q, _ = tall(qkv_ref[part[0]])
        _, k = tall(qkv_ref[part[1]])
        for start in range(0, length, block):
            end = start + block
            cols = slice(start, end)
            s = dot(k[:end], q[:, cols], 1, 0) * SCALE + bias_ref[:end, cols]
            top = jnp.max(s, axis=0, keepdims=True)
            e = jnp.exp(s - top)
            total = jnp.sum(e, axis=0, keepdims=True)
            p = (e * (1.0 / total)).astype(BF16)
            ctx_ref[part[0], cols] = dot(v[:, :end], p, 1, 0).astype(BF16)
            lse_ref[head : head + 1, cols] = top + jnp.log(total)


def fill_bias(code_ref, doc_ref, bias_ref):
    length = bias_ref.shape[0]
    block = min(256, length)
    for start in range(0, length, block):
        u = start + lax.broadcasted_iota(jnp.int32, (block, length), 0)
        t = lax.broadcasted_iota(jnp.int32, (block, length), 1)
        same = code_ref[start : start + block, :] == doc_ref[...]
        allow = ((u <= t) & same) | (u == t)
        bias_ref[start : start + block, :] = jnp.where(allow, 0.0, NEG)


def attend_back_kernel(code_ref, doc_ref, qkv_ref, lse_ref, grad_ref, out_ref, bias_ref, acc_ref):
    length = qkv_ref.shape[-1]
    heads = qkv_ref.shape[0] // (3 * HD)
    block = min(256, length)
    fill_bias(code_ref, doc_ref, bias_ref)
    for head in range(heads):
        part = [slice((i * heads + head) * HD, (i * heads + head + 1) * HD) for i in range(3)]
        q, kt, g = qkv_ref[part[0]], qkv_ref[part[1]], grad_ref[part[0]]
        q_wide, _ = tall(q)
        g_wide, _ = tall(g)
        _, k = tall(kt)
        _, v = tall(qkv_ref[part[2]])
        acc_ref[...] = jnp.zeros_like(acc_ref)
        for start in range(0, length, block):
            end = start + block
            cols = slice(start, end)
            s = dot(k[:end], q_wide[:, cols], 1, 0) * SCALE + bias_ref[:end, cols]
            p = jnp.exp(s - lse_ref[head : head + 1, cols])
            dp = dot(v[:end], g_wide[:, cols], 1, 0)
            inner = jnp.sum(p * dp, axis=0, keepdims=True)
            ds = (p * (dp - inner)).astype(BF16)
            out_ref[part[0], cols] = (dot(kt[:, :end], ds, 1, 0) * SCALE).astype(BF16)
            acc_ref[0, :, :end] += dot(q[:, cols], ds, 1, 1)
            acc_ref[1, :, :end] += dot(g[:, cols], p.astype(BF16), 1, 1)
        out_ref[part[1]] = (acc_ref[0] * SCALE).astype(BF16)
        out_ref[part[2]] = acc_ref[1].astype(BF16)


def attend(code, doc, qkv):
    heads, length = qkv.shape[0] // (3 * HD), qkv.shape[1]
    return pl.pallas_call(
        attend_kernel,
        out_shape=[
            jax.ShapeDtypeStruct((heads * HD, length), BF16),
            jax.ShapeDtypeStruct((heads, length), F32),
        ],
        scratch_shapes=[pltpu.VMEM((length, length), F32)],
        compiler_params=pltpu.CompilerParams(vmem_limit_bytes=VMEM_LIMIT),
        cost_estimate=pl.CostEstimate(
            flops=heads * length * length * HD * 4,
            bytes_accessed=heads * HD * length * 8,
            transcendentals=heads * length * length,
        ),
    )(code, doc, qkv)


def attend_back(code, doc, qkv, lse, grad):
    heads, length = qkv.shape[0] // (3 * HD), qkv.shape[1]
    return pl.pallas_call(
        attend_back_kernel,
        out_shape=jax.ShapeDtypeStruct(qkv.shape, BF16),
        scratch_shapes=[pltpu.VMEM((length, length), F32), pltpu.VMEM((2, HD, length), F32)],
        compiler_params=pltpu.CompilerParams(vmem_limit_bytes=VMEM_LIMIT),
        cost_estimate=pl.CostEstimate(
            flops=heads * length * length * HD * 10,
            bytes_accessed=heads * HD * length * 14,
            transcendentals=heads * length * length,
        ),
    )(code, doc, qkv, lse, grad)


def table_kernel(alpha_ref, eta_ref, keep_ref, table_ref, state_ref):
    spans = table_ref.shape[0]
    place = lax.broadcasted_iota(jnp.int32, (1, table_ref.shape[1]), 1)
    state = jnp.zeros((1, table_ref.shape[1]), F32)
    memory = jnp.zeros((1, table_ref.shape[1]), F32)
    for c in range(spans):
        kept = keep_ref[c : c + 1, :]
        table_ref[c : c + 1, :] = memory * kept
        state_ref[c : c + 1, :] = state * kept
        state = eta_ref[c : c + 1, :] * kept * state + jnp.where(place == c, 1.0, 0.0)
        memory = alpha_ref[c : c + 1, :] * kept * memory + state


def table_back_kernel(alpha_ref, eta_ref, keep_ref, table_ref, state_ref, grad_ref, out_ref, ga_ref, ge_ref):
    spans = table_ref.shape[0]
    wide = (1, table_ref.shape[1])
    grad_state = jnp.zeros(wide, F32)
    grad_memory = jnp.zeros(wide, F32)
    for c in reversed(range(spans)):
        kept = keep_ref[c : c + 1, :]
        grad_state = grad_state + grad_memory
        ga_ref[c : c + 1, :] = grad_memory * table_ref[c : c + 1, :]
        ge_ref[c : c + 1, :] = grad_state * state_ref[c : c + 1, :]
        grad_state = eta_ref[c : c + 1, :] * kept * grad_state
        grad_memory = kept * (alpha_ref[c : c + 1, :] * grad_memory + grad_ref[c : c + 1, :])
    out_ref[0] = jnp.broadcast_to(jnp.sum(ga_ref[...], axis=1, keepdims=True), out_ref.shape[1:])
    out_ref[1] = jnp.broadcast_to(jnp.sum(ge_ref[...], axis=1, keepdims=True), out_ref.shape[1:])


def span_table(alpha, eta, keep):
    spans = alpha.shape[0]
    wide = lambda v: jnp.broadcast_to(v[:, None], (spans, 128))
    square = jax.ShapeDtypeStruct((spans, 128), F32)
    args = (wide(alpha), wide(eta), wide(keep))
    table, state = pl.pallas_call(table_kernel, out_shape=[square, square])(*args)
    return table, (args, table, state)


def span_table_back(kept, grad):
    args, table, state = kept
    spans = table.shape[0]
    scratch = pltpu.VMEM((spans, 128), F32)
    grad = jnp.pad(grad, ((0, 0), (0, 128 - grad.shape[1])))
    both = pl.pallas_call(
        table_back_kernel,
        out_shape=jax.ShapeDtypeStruct((2, spans, 128), F32),
        scratch_shapes=[scratch, scratch],
    )(*args, table, state, grad)
    return both[0, :, 0], both[1, :, 0]


def norm_back(values, inverse, gain, grad):
    scaled = grad * gain
    inner = jnp.mean(values * scaled, axis=-1, keepdims=True)
    grad_values = inverse * scaled - values * inverse * inverse * inverse * inner
    grad_gain = jnp.sum(grad * values * inverse, axis=0)
    return grad_values, grad_gain


def inverse_of(values):
    return lax.rsqrt(jnp.mean(values * values, axis=-1, keepdims=True) + EPS)


def all_sum(plane, v):
    for axis in ("l", "h", "c"):
        v = v + swap(v, axis)
    if len(plane) == 1:
        return lax.psum(v, plane)
    for axis in ("x", "y"):
        v = v + swap(v, axis)
    return v


def all_parts(plane, v):
    for axis in ("l", "h", "c"):
        v = by_index(lax.axis_index(axis), v, swap(v, axis))
    if len(plane) == 1:
        return lax.all_gather(v, plane, axis=0, tiled=True)
    for axis in ("x", "y"):
        v = by_index(lax.axis_index(axis), v, swap(v, axis))
    return v


def on_device(
    plane,
    block_in,
    grad_out,
    resets,
    counts,
    gain_in,
    w_forget,
    w_momentum,
    project_in,
    project_out,
    memory_in,
    memory_out,
    gain_mid,
    gate_weight,
    up_weight,
    down_weight,
):
    relative = functools.partial(shuffle, plane)
    absolute = functools.partial(shuffle, plane, back=True)
    c, l = lax.axis_index("c"), lax.axis_index("l")
    quarter, width = block_in.shape
    length = 4 * quarter
    spans = length // CH
    own_spans = quarter // CH
    member = 2 * c + l
    hidden_units = 4 * memory_in.shape[1]
    units, q_cols, ff = memory_in.shape[1] // 2, project_in.shape[2] // 2, gate_weight.shape[1] // 2

    x_own = relative(turn(block_in))
    flags = turn(cat([resets, counts[:, None]], 1))
    packed = [
        pack([memory_in, project_in[0], project_in[1], project_in[2]]),
        pack([memory_out.T, project_out.T]),
        pack([gate_weight, up_weight, down_weight.T]),
    ]
    far = [swap(packed[0], "h")]
    far.append(swap(after(packed[1], far[0]), "h"))
    far.append(swap(after(packed[2], far[1]), "h"))
    stages = [
        (packed[0], "x"),
        (packed[1], "y"),
        (far[0], "x"),
        (far[1], "y"),
        (packed[2], "x"),
        (far[2], "y"),
    ]
    weights, done = [], None
    for piece, first in stages:
        whole, done = gather_plane(plane, piece if done is None else after(piece, done), first)
        weights.append(whole)
    first_layer, second_layer, feed = (
        (weights[0], weights[2]),
        (weights[1], weights[3]),
        (weights[4], weights[5]),
    )
    both = range(2)

    x_full = gather_rows(x_own)
    vectors = cat([v[None] for v in (gain_in, w_forget, w_momentum, gain_mid)], 0).astype(F32)
    vectors = all_parts(plane, vectors[None])
    vectors = relative(jnp.swapaxes(vectors, 0, 1).reshape(4, width))
    gain_one, gain_two, gates = vectors[0], vectors[3], vectors[1:3]

    resets, count = flags[0, :-1], flags[0, -1]
    positions = jnp.arange(length, dtype=jnp.int32)
    valid = (positions < count).astype(F32)
    keep = (1 - resets).astype(F32)
    doc = jnp.repeat(jnp.cumsum(resets, dtype=jnp.int32), CH).astype(F32)
    code = jnp.where(valid > 0, doc, -1.0)[:, None]
    doc = doc[None, :]

    x_wide = x_full.astype(F32)
    normed = (x_wide * inverse_of(x_wide) * gain_one).astype(BF16)
    x_own = x_own.astype(F32)
    inverse_one = inverse_of(x_own)
    span_sums = jnp.sum(normed.reshape(spans, CH, width).astype(F32), axis=1)
    logits = jnp.sum(span_sums[None] * gates[:, None, :], axis=2) / CH
    alpha = jax.nn.sigmoid(logits[0] + ALPHA_SHIFT)
    eta = jax.nn.sigmoid(logits[1] + ETA_SHIFT)
    table, kept_table = span_table(alpha, eta, keep)

    act, slope_pre, qkv, ctx, lse = [], [], [], [], []
    for i in both:
        pre = dot(normed, first_layer[i][:, :units], 1, 0)
        sig_pre = jax.nn.sigmoid(pre)
        act.append((pre * sig_pre).astype(BF16))
        slope_pre.append((sig_pre * (1.0 + pre * (1.0 - sig_pre))).astype(BF16))
        qkv.append(dot(first_layer[i][:, units:], normed, 0, 1).astype(BF16))
    sim = scatter_rows((dot(act[0], act[0], 1, 1) + dot(act[1], act[1], 1, 1)) / hidden_units)
    for i in both:
        context, logsum = attend(code, doc, qkv[i])
        ctx.append(context)
        lse.append(logsum)
    out_own = scatter_rows(
        sum(dot(act[i], second_layer[i][:, :units], 1, 1) for i in both)
        + sum(dot(ctx[i], second_layer[i][:, units:], 0, 1) for i in both)
    )
    table_own = lax.dynamic_slice_in_dim(table[:, :spans], member * own_spans, own_spans, 0)
    spread = jnp.repeat(jnp.repeat(table_own, CH, axis=0), CH, axis=1)
    mixing = (sim * spread * valid[None, :] / CH).astype(BF16)
    middle = x_own + out_own + dot(mixing, normed, 1, 0)
    inverse_two = inverse_of(middle)
    mid = (middle * inverse_two * gain_two).astype(BF16)
    mid_all = gather_rows(mid)
    grad_own = relative(turn(grad_out))
    grad_all = gather_rows(grad_own)

    hidden, grad_gate_pre, grad_up_pre = [], [], []
    for i in both:
        gate = dot(mid_all, feed[i][:, :ff], 1, 0)
        up = dot(mid_all, feed[i][:, ff : 2 * ff], 1, 0)
        grad_hidden = dot(grad_all, feed[i][:, 2 * ff :], 1, 0)
        sigma = jax.nn.sigmoid(gate)
        swish = gate * sigma
        hidden.append((swish * up).astype(BF16))
        grad_gate_pre.append((grad_hidden * up * (sigma * (1.0 + gate * (1.0 - sigma)))).astype(BF16))
        grad_up_pre.append((grad_hidden * swish).astype(BF16))
    grad_mid = scatter_rows(
        sum(
            dot(grad_gate_pre[i], feed[i][:, :ff], 1, 1) + dot(grad_up_pre[i], feed[i][:, ff : 2 * ff], 1, 1)
            for i in both
        )
    )
    ffn_own = scatter_rows(sum(dot(hidden[i], feed[i][:, 2 * ff :], 1, 1) for i in both))
    block_out = turn(absolute((middle + ffn_own).astype(BF16)))
    grad_gate, grad_up, grad_down = reduce_group(
        plane, [(mid_all, *grad_gate_pre), (mid_all, *grad_up_pre), (grad_all, *hidden)]
    )

    back_two, grad_gain_two = norm_back(middle, inverse_two, gain_two, grad_mid)
    grad_middle = grad_own.astype(F32) + back_two
    branch = grad_middle.astype(BF16)
    branch_all = gather_rows(branch)
    scaled = dot(branch, normed, 1, 1) / CH * valid[None, :]
    grad_sim = gather_rows((scaled * spread).astype(BF16))
    grad_blocks = jnp.sum((scaled * sim).reshape(own_spans, CH, spans, CH), axis=(1, 3))
    grad_table = lax.dynamic_update_slice_in_dim(
        jnp.zeros((spans, spans), F32), grad_blocks, member * own_spans, 0
    )
    for axis in ("c", "l"):
        grad_table = grad_table + swap(grad_table, axis)
    grad_alpha, grad_eta = span_table_back(kept_table, grad_table)
    grad_logits = jnp.stack([grad_alpha * alpha * (1.0 - alpha), grad_eta * eta * (1.0 - eta)]) / CH
    grad_vectors = jnp.sum(grad_logits[:, :, None] * span_sums[None], axis=1)
    own_logits = lax.dynamic_slice_in_dim(grad_logits, member * own_spans, own_spans, 1)
    grad_spans = jnp.sum(own_logits[:, :, None] * gates[:, None, :], axis=0)

    grad_memory_out, grad_project_out = reduce_group(
        plane, [(branch_all, *act), (branch_all, ctx[0].T, ctx[1].T)]
    )
    symmetric = (grad_sim.astype(F32) + grad_sim.T.astype(F32)).astype(BF16)
    grad_pre, grad_qkv = [], []
    for i in both:
        grad_act = (
            dot(branch_all, second_layer[i][:, :units], 1, 0) + dot(symmetric, act[i], 1, 0) / hidden_units
        )
        grad_pre.append((grad_act * slope_pre[i].astype(F32)).astype(BF16))
    (grad_memory_in,) = reduce_group(plane, [(normed, *grad_pre)])
    for i in both:
        grad_ctx = dot(second_layer[i][:, units:], branch_all, 0, 1).astype(BF16)
        grad_qkv.append(attend_back(code, doc, qkv[i], lse[i], grad_ctx))
    (grad_qkv_sum,) = reduce_group(plane, [(normed, grad_qkv[0].T, grad_qkv[1].T)])
    grad_normed = scatter_rows(
        dot(mixing, branch, 0, 0)
        + sum(
            dot(grad_pre[i], first_layer[i][:, :units], 1, 1)
            + dot(grad_qkv[i], first_layer[i][:, units:], 0, 1)
            for i in both
        )
    )
    grad_normed = grad_normed + jnp.repeat(grad_spans, CH, axis=0)
    back_one, grad_gain_one = norm_back(x_own, inverse_one, gain_one, grad_normed)
    grad_block_in = turn(absolute((grad_middle + back_one).astype(BF16))).astype(F32)

    gram = 0.0
    for i in both:
        blocks = act[i].reshape(spans, CH, -1)
        gram = gram + jnp.einsum("cth,csh->cts", blocks, blocks, preferred_element_type=F32)
    written = (normed * valid[:, None].astype(BF16)).reshape(spans, CH, width)
    cross = jnp.einsum("ctd,csd->cts", written, written, preferred_element_type=F32)
    piece = jnp.sum(gram * cross, axis=(1, 2))
    for axis in ("c", "l"):
        piece = piece + swap(piece, axis)
    surprise = jnp.sqrt(piece / (hidden_units * width * CH))
    weight = jnp.sum(valid.reshape(spans, CH), axis=1)
    numbers = jnp.stack(
        [jnp.sum(weight * surprise), jnp.sum(weight * alpha), jnp.sum(weight * eta), jnp.sum(weight)]
    )
    small = jnp.stack([grad_gain_one, grad_vectors[0] * 0.25, grad_vectors[1] * 0.25, grad_gain_two])
    small = cat([absolute(small), jnp.pad(numbers[None], ((0, 0), (0, width - 4)))], 0)
    small = all_sum(plane, small)
    logged = small[4, :3] / small[4, 3]
    share = gain_in.shape[0]
    index = lax.axis_index(plane + ("c", "h", "l"))
    mine = lax.dynamic_slice_in_dim(small, index * share, share, 1)
    grad_project_in = jnp.stack(
        [
            cat([grad_qkv_sum[:, (3 * j + i) * q_cols : (3 * j + i + 1) * q_cols] for j in both], 1)
            for i in range(3)
        ]
    )
    return (
        block_out,
        grad_block_in,
        mine[0],
        mine[1],
        mine[2],
        grad_project_in,
        grad_project_out.T,
        grad_memory_in,
        grad_memory_out.T,
        mine[3],
        grad_gate,
        grad_up,
        grad_down.T,
        logged,
    )


def solution(mesh):
    chips, line = mesh.shape["dp"] // 2, mesh.shape["mp"]
    if chips == 4:
        plane, sizes = ("y", "x"), (2, 2)
    else:
        plane, sizes = ("p",), (chips,)
    fine = Mesh(mesh.devices.reshape(sizes + (2, line // 2, 2)), plane + ("c", "h", "l"))
    dp, mp = plane + ("c",), ("h", "l")
    every = dp + mp
    placed = (
        P(every, None),
        P(every, None),
        P(dp, None),
        P(dp),
        P(every),
        P(every),
        P(every),
        P(None, dp, mp),
        P(mp, dp),
        P(dp, mp),
        P(mp, dp),
        P(every),
        P(dp, mp),
        P(dp, mp),
        P(mp, dp),
    )
    return jax.shard_map(
        functools.partial(on_device, plane),
        mesh=fine,
        in_specs=placed,
        out_specs=(
            P(every, None),
            P(every, None),
            P(every),
            P(every),
            P(every),
            P(None, dp, mp),
            P(mp, dp),
            P(dp, mp),
            P(mp, dp),
            P(every),
            P(dp, mp),
            P(dp, mp),
            P(mp, dp),
            P(),
        ),
        check_vma=False,
    )
```

```python
import functools

import jax
import jax.numpy as jnp
from jax import lax
from jax.experimental import pallas as pl
from jax.experimental.layout import Layout, with_layout_constraint
from jax.experimental.pallas import tpu as pltpu
from jax.sharding import Mesh
from jax.sharding import PartitionSpec as P

HD = 96
CH = 64
EPS = 1e-06
ALPHA_SHIFT = 1.5
ETA_SHIFT = 0.5
NEG = -1e30
SCALE = HD ** (-0.5)
F32 = jnp.float32
BF16 = jnp.bfloat16
VMEM_LIMIT = 24 * 1024 * 1024

def dot(a, b, ca, cb):
    return lax.dot_general(a, b, (((ca,), (cb,)), ((), ())), preferred_element_type=F32)


def swap(x, axis):
    return lax.ppermute(x, axis, [(0, 1), (1, 0)])


def turn(x):
    return lax.ppermute(x, ("c", "h"), [(0, 0), (1, 2), (2, 1), (3, 3)])


def after(x, *others):
    if isinstance(x, (list, tuple)):
        return list(lax.optimization_barrier((*x, *others))[: len(x)])
    return lax.optimization_barrier((x, *others))[0]


def cat(parts, axis=0):
    return jnp.concatenate(parts, axis=axis)


def by_rows(x):
    return with_layout_constraint(x, Layout(major_to_minor=tuple(range(x.ndim))))


def by_index(index, first, second, axis=0):
    return cat([jnp.where(index == 0, first, second), jnp.where(index == 0, second, first)], axis)


def gather_rows(x):
    c, l = lax.axis_index("c"), lax.axis_index("l")
    half = by_index(l, x, swap(x, "l"))
    return by_index(c, half, swap(half, "c"))


class RowSum:
    def __init__(self, x):
        c = lax.axis_index("c")
        rows = x.shape[0] // 2
        self.sent = lax.dynamic_slice_in_dim(x, (1 - c) * rows, rows, 0).astype(BF16)
        self.kept = lax.dynamic_slice_in_dim(x, c * rows, rows, 0)

    def cores(self):
        l = lax.axis_index("l")
        half = self.kept.astype(F32) + swap(self.sent, "c").astype(F32)
        rows = half.shape[0] // 2
        self.sent = lax.dynamic_slice_in_dim(half, (1 - l) * rows, rows, 0).astype(BF16)
        self.kept = lax.dynamic_slice_in_dim(half, l * rows, rows, 0)

    def chips(self):
        return self.kept + swap(self.sent, "l").astype(F32)


def shuffle(plane, v, back=False):
    if len(plane) == 1:
        return v
    share = v.shape[-1] // 4
    b = [v[..., i * share : (i + 1) * share] for i in range(4)]
    if back:
        b = [b[0], b[1], b[3], b[2]]
    x, y = lax.axis_index("x"), lax.axis_index("y")
    b = [jnp.where(x == 0, b[i], b[i ^ 1]) for i in range(4)]
    b = [jnp.where(y == 0, b[i], b[i ^ 2]) for i in range(4)]
    if not back:
        b = [b[0], b[1], b[3], b[2]]
    return cat(b, -1)


class PlaneGather:
    def __init__(self, plane, piece, first):
        if len(plane) == 1:
            self.parts = [lax.all_gather(piece, plane, axis=0, tiled=True)]
            self.near, self.far = self.parts, self.parts[0]
            return
        near = {axis: swap(piece, axis) for axis in plane}
        second = "y" if first == "x" else "x"
        self.far = swap(near[first], second)
        self.near = [near["x"], near["y"]]
        self.parts = [piece, near["x"], self.far, near["y"]]

    def whole(self):
        return by_rows(cat(self.parts) if len(self.parts) > 1 else self.parts[0])


class PlaneSum:
    def __init__(self, plane, pairs, first):
        self.plane, self.pairs, self.first = plane, pairs, first
        width = pairs[0][0].shape[1]
        self.w = w = width // 4
        if len(plane) == 1:
            self.sent = self.product(0, width)
        elif first == "x":
            self.sent = self.product(w, 3 * w)
        else:
            self.sent = self.product(2 * w, 4 * w)

    def product(self, start, stop):
        parts = [dot(left[:, start:stop], right, 0, 0).astype(BF16) for left, right in self.pairs]
        return cat(parts, 1) if len(parts) > 1 else parts[0]

    def second(self, ties=()):
        if len(self.plane) == 1:
            self.total = lax.psum_scatter(self.sent, self.plane, scatter_dimension=0, tiled=True).astype(F32)
            self.sent = self.got = self.total
            return
        w = self.w
        self.got = got = after(swap(self.sent, self.first), *ties)
        if self.first == "x":
            self.axis, mine, other, other_at = "y", got[:w], got[w:], 3
        else:
            self.axis, mine, other, other_at = "x", got[w:], got[:w], 1
        other = self.product(other_at * w, (other_at + 1) * w).astype(F32) + other.astype(F32)
        self.sent = other.astype(BF16)
        self.total = self.product(0, w).astype(F32) + mine.astype(F32)

    def last(self):
        if len(self.plane) > 1:
            self.total = self.total + swap(self.sent, self.axis).astype(F32)


class GroupSum:
    def __init__(self, plane, sources):
        self.columns = [right.shape[1] for _, right, _ in sources]
        self.here = PlaneSum(plane, [(left, right) for left, right, _ in sources], "x")
        self.there = PlaneSum(plane, [(left, right) for left, _, right in sources], "y")
        self.sent = [self.here.sent, self.there.sent]

    def second(self, ties=()):
        self.here.second(ties)
        self.there.second(ties)
        self.sent = [self.here.sent, self.there.sent]

    def line(self):
        self.there.last()
        self.sent = [self.there.total.astype(BF16)]
        self.here.last()
        self.sent.append(self.here.total)

    def cores(self, ties=()):
        got = swap(self.sent[0], "h")
        mine = self.here.total + (after(got, *ties) if ties else got).astype(F32)
        c = lax.axis_index("c")
        rows = mine.shape[0] // 2
        self.given = lax.dynamic_slice_in_dim(mine, (1 - c) * rows, rows, 0).astype(BF16)
        self.kept = lax.dynamic_slice_in_dim(mine, c * rows, rows, 0)

    def results(self):
        c = lax.axis_index("c")
        got = swap(self.given, "c").astype(F32)
        results, start = [], 0
        for n in self.columns:
            results.append(by_index(c, self.kept[:, start : start + n], got[:, start : start + n], 1))
            start += n
        return results


def pack(groups, common=()):
    c = lax.axis_index("c")
    mine, other, results, start = [], [], [], 0
    for shards in groups:
        columns = sum(s.shape[1] // 2 for s in shards) + sum(s.shape[1] for s in common)
        filled = list(common)
        if columns % 128:
            filled.append(jnp.zeros((shards[0].shape[0], 128 - columns % 128), BF16))
        low = cat([s[:, : s.shape[1] // 2] for s in shards] + filled, 1)
        high = cat([s[:, s.shape[1] // 2 :] for s in shards] + filled, 1)
        mine.append(jnp.where(c == 0, low, high))
        other.append(jnp.where(c == 0, high, low))
    got = swap(cat(other, 1), "c")
    for block in mine:
        results.append(by_rows(by_index(c, block, got[:, start : start + block.shape[1]])))
        start += block.shape[1]
    return results


def tall(x):
    padding = 128 - x.shape[0]
    wide = cat([x.astype(F32), jnp.zeros((padding, x.shape[1]), F32)])
    return wide.astype(BF16), wide.T.astype(BF16)


def attend_kernel(code_ref, doc_ref, qkv_ref, ctx_ref, lse_ref, bias_ref):
    length = qkv_ref.shape[-1]
    heads = qkv_ref.shape[0] // (3 * HD)
    block = min(256, length)
    fill_bias(code_ref, doc_ref, bias_ref)
    for head in range(heads):
        part = [slice((i * heads + head) * HD, (i * heads + head + 1) * HD) for i in range(3)]
        v = qkv_ref[part[2]]
        q, _ = tall(qkv_ref[part[0]])
        _, k = tall(qkv_ref[part[1]])
        for start in range(0, length, block):
            end = start + block
            cols = slice(start, end)
            s = dot(k[:end], q[:, cols], 1, 0) * SCALE + bias_ref[:end, cols]
            top = jnp.max(s, axis=0, keepdims=True)
            e = jnp.exp(s - top)
            total = jnp.sum(e, axis=0, keepdims=True)
            p = (e * (1.0 / total)).astype(BF16)
            ctx_ref[part[0], cols] = dot(v[:, :end], p, 1, 0).astype(BF16)
            lse_ref[head : head + 1, cols] = top + jnp.log(total)


def sum_kernel(terms, weights, *refs):
    weight_refs, left_refs, out_ref = refs[:weights], refs[weights:-1], refs[-1]
    total = None
    for (which, start, stop, side), left_ref in zip(terms, left_refs):
        right = weight_refs[which][:, start:stop]
        part = dot(left_ref[...], right, side, 1)
        total = part if total is None else total + part
    out_ref[...] = total.astype(BF16)


def sum_dots(weights, terms):
    left, side = terms[0][0], terms[0][4]
    rows, width = left.shape[1 - side], weights[0].shape[0]
    tile, wide = min(512, rows), 512
    in_specs = [pl.BlockSpec((wide, w.shape[1]), lambda n, m: (n, 0)) for w in weights]
    for left, _, _, _, side in terms:
        if side == 1:
            in_specs.append(pl.BlockSpec((tile, left.shape[1]), lambda n, m: (m, 0)))
        else:
            in_specs.append(pl.BlockSpec((left.shape[0], tile), lambda n, m: (0, m)))
    return pl.pallas_call(
        functools.partial(sum_kernel, [t[1:] for t in terms], len(weights)),
        grid=(width // wide, rows // tile),
        in_specs=in_specs,
        out_specs=pl.BlockSpec((tile, wide), lambda n, m: (m, n)),
        out_shape=jax.ShapeDtypeStruct((rows, width), BF16),
        compiler_params=pltpu.CompilerParams(vmem_limit_bytes=VMEM_LIMIT),
        cost_estimate=pl.CostEstimate(
            flops=2 * rows * width * sum(t[3] - t[2] for t in terms),
            bytes_accessed=2 * sum(w.size for w in weights) + 8 * sum(t[0].size for t in terms),
            transcendentals=0,
        ),
    )(*weights, *[t[0] for t in terms])


def fill_bias(code_ref, doc_ref, bias_ref):
    length = bias_ref.shape[0]
    block = min(256, length)
    for start in range(0, length, block):
        u = start + lax.broadcasted_iota(jnp.int32, (block, length), 0)
        t = lax.broadcasted_iota(jnp.int32, (block, length), 1)
        same = code_ref[start : start + block, :] == doc_ref[...]
        allow = ((u <= t) & same) | (u == t)
        bias_ref[start : start + block, :] = jnp.where(allow, 0.0, NEG)


def attend_back_kernel(code_ref, doc_ref, qkv_ref, lse_ref, grad_ref, out_ref, bias_ref, acc_ref):
    length = qkv_ref.shape[-1]
    heads = qkv_ref.shape[0] // (3 * HD)
    block = min(256, length)
    fill_bias(code_ref, doc_ref, bias_ref)
    for head in range(heads):
        part = [slice((i * heads + head) * HD, (i * heads + head + 1) * HD) for i in range(3)]
        q, kt, g = qkv_ref[part[0]], qkv_ref[part[1]], grad_ref[part[0]]
        q_wide, _ = tall(q)
        g_wide, _ = tall(g)
        _, k = tall(kt)
        _, v = tall(qkv_ref[part[2]])
        acc_ref[...] = jnp.zeros_like(acc_ref)
        for start in range(0, length, block):
            end = start + block
            cols = slice(start, end)
            s = dot(k[:end], q_wide[:, cols], 1, 0) * SCALE + bias_ref[:end, cols]
            p = jnp.exp(s - lse_ref[head : head + 1, cols])
            dp = dot(v[:end], g_wide[:, cols], 1, 0)
            inner = jnp.sum(p * dp, axis=0, keepdims=True)
            ds = (p * (dp - inner)).astype(BF16)
            out_ref[part[0], cols] = (dot(kt[:, :end], ds, 1, 0) * SCALE).astype(BF16)
            acc_ref[0, :, :end] += dot(q[:, cols], ds, 1, 1)
            acc_ref[1, :, :end] += dot(g[:, cols], p.astype(BF16), 1, 1)
        out_ref[part[1]] = (acc_ref[0] * SCALE).astype(BF16)
        out_ref[part[2]] = acc_ref[1].astype(BF16)


def attend(code, doc, qkv):
    heads, length = qkv.shape[0] // (3 * HD), qkv.shape[1]
    return pl.pallas_call(
        attend_kernel,
        out_shape=[
            jax.ShapeDtypeStruct((heads * HD, length), BF16),
            jax.ShapeDtypeStruct((heads, length), F32),
        ],
        scratch_shapes=[pltpu.VMEM((length, length), F32)],
        compiler_params=pltpu.CompilerParams(vmem_limit_bytes=VMEM_LIMIT),
        cost_estimate=pl.CostEstimate(
            flops=heads * length * length * HD * 4,
            bytes_accessed=heads * HD * length * 8,
            transcendentals=heads * length * length,
        ),
    )(code, doc, qkv)


def attend_back(code, doc, qkv, lse, grad):
    heads, length = qkv.shape[0] // (3 * HD), qkv.shape[1]
    return pl.pallas_call(
        attend_back_kernel,
        out_shape=jax.ShapeDtypeStruct(qkv.shape, BF16),
        scratch_shapes=[pltpu.VMEM((length, length), F32), pltpu.VMEM((2, HD, length), F32)],
        compiler_params=pltpu.CompilerParams(vmem_limit_bytes=VMEM_LIMIT),
        cost_estimate=pl.CostEstimate(
            flops=heads * length * length * HD * 10,
            bytes_accessed=heads * HD * length * 14,
            transcendentals=heads * length * length,
        ),
    )(code, doc, qkv, lse, grad)


def table_kernel(alpha_ref, eta_ref, keep_ref, table_ref, state_ref):
    spans = table_ref.shape[0]
    place = lax.broadcasted_iota(jnp.int32, (1, table_ref.shape[1]), 1)
    state = jnp.zeros((1, table_ref.shape[1]), F32)
    memory = jnp.zeros((1, table_ref.shape[1]), F32)
    for c in range(spans):
        kept = keep_ref[c : c + 1, :]
        table_ref[c : c + 1, :] = memory * kept
        state_ref[c : c + 1, :] = state * kept
        state = eta_ref[c : c + 1, :] * kept * state + jnp.where(place == c, 1.0, 0.0)
        memory = alpha_ref[c : c + 1, :] * kept * memory + state


def table_back_kernel(alpha_ref, eta_ref, keep_ref, table_ref, state_ref, grad_ref, out_ref, ga_ref, ge_ref):
    spans = table_ref.shape[0]
    wide = (1, table_ref.shape[1])
    grad_state = jnp.zeros(wide, F32)
    grad_memory = jnp.zeros(wide, F32)
    for c in reversed(range(spans)):
        kept = keep_ref[c : c + 1, :]
        grad_state = grad_state + grad_memory
        ga_ref[c : c + 1, :] = grad_memory * table_ref[c : c + 1, :]
        ge_ref[c : c + 1, :] = grad_state * state_ref[c : c + 1, :]
        grad_state = eta_ref[c : c + 1, :] * kept * grad_state
        grad_memory = kept * (alpha_ref[c : c + 1, :] * grad_memory + grad_ref[c : c + 1, :])
    out_ref[0] = jnp.broadcast_to(jnp.sum(ga_ref[...], axis=1, keepdims=True), out_ref.shape[1:])
    out_ref[1] = jnp.broadcast_to(jnp.sum(ge_ref[...], axis=1, keepdims=True), out_ref.shape[1:])


def span_table(alpha, eta, keep):
    spans = alpha.shape[0]
    wide = lambda v: jnp.broadcast_to(v[:, None], (spans, 128))
    square = jax.ShapeDtypeStruct((spans, 128), F32)
    args = (wide(alpha), wide(eta), wide(keep))
    table, state = pl.pallas_call(table_kernel, out_shape=[square, square])(*args)
    return table, (args, table, state)


def span_table_back(kept, grad):
    args, table, state = kept
    spans = table.shape[0]
    scratch = pltpu.VMEM((spans, 128), F32)
    grad = jnp.pad(grad, ((0, 0), (0, 128 - grad.shape[1])))
    both = pl.pallas_call(
        table_back_kernel,
        out_shape=jax.ShapeDtypeStruct((2, spans, 128), F32),
        scratch_shapes=[scratch, scratch],
    )(*args, table, state, grad)
    return both[0, :, 0], both[1, :, 0]


def norm_back(values, inverse, gain, grad):
    scaled = grad * gain
    inner = jnp.mean(values * scaled, axis=-1, keepdims=True)
    grad_values = inverse * scaled - values * inverse * inverse * inverse * inner
    grad_gain = jnp.sum(grad * values * inverse, axis=0)
    return grad_values, grad_gain


def inverse_of(values):
    return lax.rsqrt(jnp.mean(values * values, axis=-1, keepdims=True) + EPS)


def all_sum(plane, v):
    for axis in ("l", "h", "c"):
        v = v + swap(v, axis)
    if len(plane) == 1:
        return lax.psum(v, plane)
    for axis in ("x", "y"):
        v = v + swap(v, axis)
    return v


def all_parts(plane, v):
    for axis in ("l", "h", "c"):
        v = by_index(lax.axis_index(axis), v, swap(v, axis))
    if len(plane) == 1:
        return lax.all_gather(v, plane, axis=0, tiled=True)
    for axis in ("x", "y"):
        v = by_index(lax.axis_index(axis), v, swap(v, axis))
    return v


def on_device(
    plane,
    block_in,
    grad_out,
    resets,
    counts,
    gain_in,
    w_forget,
    w_momentum,
    project_in,
    project_out,
    memory_in,
    memory_out,
    gain_mid,
    gate_weight,
    up_weight,
    down_weight,
):
    relative = functools.partial(shuffle, plane)
    absolute = functools.partial(shuffle, plane, back=True)
    c, l = lax.axis_index("c"), lax.axis_index("l")
    quarter, width = block_in.shape
    length = 4 * quarter
    spans = length // CH
    own_spans = quarter // CH
    member = 2 * c + l
    hidden_units = 4 * memory_in.shape[1]
    units, q_cols, ff = memory_in.shape[1] // 2, project_in.shape[2] // 2, gate_weight.shape[1] // 2

    vectors = cat([v[None] for v in (gain_in, w_forget, w_momentum, gain_mid)], 0)
    for axis in ("l", "h"):
        vectors = by_index(lax.axis_index(axis), vectors, swap(vectors, axis), 1)
    first = [memory_in, project_in[0], project_in[1], project_in[2]]
    x_turned = turn(block_in)
    flags = turn(cat([resets, counts[:, None]], 1))
    (share0,) = pack([first], [vectors.T])
    far0 = swap(after(share0, x_turned), "h")
    late = after([memory_out.T, project_out.T, gate_weight, up_weight, down_weight.T], share0)
    share1, share2 = pack([late[:2], late[2:]])
    x_own = relative(x_turned)
    half = by_index(l, x_own, swap(x_own, "l"))
    other_half = swap(half, "c")
    x_full = by_index(c, half, other_half)
    stages = [PlaneGather(plane, share0, "x")]
    share1 = after(share1, *stages[0].near)
    stages.append(PlaneGather(plane, share1, "y"))
    far0 = after(far0, *stages[0].near)
    stages.append(PlaneGather(plane, far0, "x"))
    far1 = swap(after(share1, far0), "h")
    far1 = after(far1, *stages[2].near, *stages[1].near)
    grad_turned = turn(after(grad_out, far1))
    stages.append(PlaneGather(plane, far1, "y"))
    far2 = swap(after(share2, far1), "h")
    share2 = after(share2, *stages[3].near, stages[1].far, stages[2].far, grad_turned)
    stages.append(PlaneGather(plane, share2, "x"))
    far2 = after(far2, *stages[4].near, stages[3].far)
    stages.append(PlaneGather(plane, far2, "y"))
    first_layer, second_layer, feed = (
        [stages[i].whole(), stages[j].whole()] for i, j in ((0, 2), (1, 3), (4, 5))
    )
    both = range(2)
    q_end = units + 3 * q_cols
    out_end = units + q_cols
    vectors = first_layer[0][:, q_end : q_end + 4].T.astype(F32)
    gain_one, gain_two, gates = vectors[0], vectors[3], vectors[1:3]

    resets, count = flags[0, :-1], flags[0, -1]
    positions = jnp.arange(length, dtype=jnp.int32)
    valid = (positions < count).astype(F32)
    keep = (1 - resets).astype(F32)
    doc = jnp.repeat(jnp.cumsum(resets, dtype=jnp.int32), CH).astype(F32)
    code = jnp.where(valid > 0, doc, -1.0)[:, None]
    doc = doc[None, :]

    x_wide = x_full.astype(F32)
    normed = (x_wide * inverse_of(x_wide) * gain_one).astype(BF16)
    x_own = x_own.astype(F32)
    inverse_one = inverse_of(x_own)
    span_sums = jnp.sum(normed.reshape(spans, CH, width).astype(F32), axis=1)
    logits = jnp.sum(span_sums[None] * gates[:, None, :], axis=2) / CH
    alpha = jax.nn.sigmoid(logits[0] + ALPHA_SHIFT)
    eta = jax.nn.sigmoid(logits[1] + ETA_SHIFT)
    table, kept_table = span_table(alpha, eta, keep)

    act, slope_pre, qkv, ctx, lse = [], [], [], [], []
    for i in both:
        pre = dot(normed, first_layer[i][:, :units], 1, 0)
        sig_pre = jax.nn.sigmoid(pre)
        act.append((pre * sig_pre).astype(BF16))
        slope_pre.append((sig_pre * (1.0 + pre * (1.0 - sig_pre))).astype(BF16))
        qkv.append(dot(first_layer[i][:, units:q_end], normed, 0, 1).astype(BF16))
    sim_sum = RowSum((dot(act[0], act[0], 1, 1) + dot(act[1], act[1], 1, 1)) / hidden_units)
    sim_sum.cores()
    sim = sim_sum.chips()
    qkv[1] = after(qkv[1], *stages[4].near)
    for i in both:
        context, logsum = attend(code, doc, qkv[i])
        ctx.append(context)
        lse.append(logsum)
    act_late = after(act, far2)
    out_sum = RowSum(
        sum_dots(
            second_layer,
            [(act_late[i], i, 0, units, 1) for i in both] + [(ctx[i], i, units, out_end, 0) for i in both],
        )
    )
    out_sum.cores()
    out_own = out_sum.chips()
    table_own = lax.dynamic_slice_in_dim(table[:, :spans], member * own_spans, own_spans, 0)
    spread = jnp.repeat(jnp.repeat(table_own, CH, axis=0), CH, axis=1)
    sim = after(sim, *stages[5].near)
    mixing = (sim * spread * valid[None, :] / CH).astype(BF16)
    middle = x_own + out_own + dot(mixing, normed, 1, 0)
    inverse_two = inverse_of(middle)
    mid = (middle * inverse_two * gain_two).astype(BF16)
    mid_all = gather_rows(mid)
    grad_own = relative(grad_turned)
    grad_all = gather_rows(grad_own)

    hidden, grad_gate_pre, grad_up_pre = [], [], []
    for i in both:
        gate = dot(mid_all, feed[i][:, :ff], 1, 0)
        up = dot(mid_all, feed[i][:, ff : 2 * ff], 1, 0)
        grad_hidden = dot(grad_all, feed[i][:, 2 * ff :], 1, 0)
        sigma = jax.nn.sigmoid(gate)
        swish = gate * sigma
        hidden.append((swish * up).astype(BF16))
        grad_gate_pre.append((grad_hidden * up * (sigma * (1.0 + gate * (1.0 - sigma)))).astype(BF16))
        grad_up_pre.append((grad_hidden * swish).astype(BF16))
    mid_sum = RowSum(
        sum_dots(
            feed,
            [(grad_gate_pre[i], i, 0, ff, 1) for i in both] + [(grad_up_pre[i], i, ff, 2 * ff, 1) for i in both],
        )
    )
    mid_sum.cores()
    mid_late, grad_late = after([mid_all, grad_all], mid_sum.sent)
    feed_sum = GroupSum(
        plane, [(mid_late, *grad_gate_pre), (mid_late, *grad_up_pre), (grad_late, *hidden)]
    )
    hidden = after(hidden, mid_sum.sent, *feed_sum.sent)
    ffn_sum = RowSum(sum_dots(feed, [(hidden[i], i, 2 * ff, 3 * ff, 1) for i in both]))
    grad_mid = after(mid_sum.chips(), ffn_sum.sent)

    back_two, grad_gain_two = norm_back(middle, inverse_two, gain_two, grad_mid)
    grad_middle = grad_own.astype(F32) + back_two
    branch = grad_middle.astype(BF16)
    branch_all = gather_rows(branch)
    scaled = dot(branch, normed, 1, 1) / CH * valid[None, :]
    grad_sim_own = (scaled * spread).astype(BF16)
    grad_sim = gather_rows(grad_sim_own)
    grad_blocks = jnp.sum((scaled * sim).reshape(own_spans, CH, spans, CH), axis=(1, 3))
    grad_table = lax.dynamic_update_slice_in_dim(
        jnp.zeros((spans, spans), F32), grad_blocks, member * own_spans, 0
    )

    feed_sum.second()
    branch_all = after(branch_all, *feed_sum.sent)
    out_grad_sum = GroupSum(plane, [(branch_all, *act), (branch_all, ctx[0].T, ctx[1].T)])
    branch_all = after(branch_all, *out_grad_sum.sent)
    grad_pre, grad_qkv = [], []
    for i in both:
        grad_ctx = dot(second_layer[i][:, units:out_end], branch_all, 0, 1).astype(BF16)
        grad_qkv.append(attend_back(code, doc, qkv[i], lse[i], grad_ctx))
    feed_sum.line()
    out_grad_sum.second()
    normed_late = after(normed, *feed_sum.sent, *grad_qkv, *out_grad_sum.sent)
    qkv_sum = GroupSum(plane, [(normed_late, grad_qkv[0].T, grad_qkv[1].T)])
    out_grad_sum.line()
    grad_sim, branch_late = after([grad_sim, branch_all], *qkv_sum.sent, *out_grad_sum.sent)
    symmetric = (grad_sim.astype(F32) + grad_sim.T.astype(F32)).astype(BF16)
    for i in both:
        grad_act = (
            dot(branch_late, second_layer[i][:, :units], 1, 0) + dot(symmetric, act[i], 1, 0) / hidden_units
        )
        grad_pre.append((grad_act * slope_pre[i].astype(F32)).astype(BF16))
        if i == 0:
            qkv_sum.second()
            feed_sum.cores([grad_pre[0]])
            symmetric, branch_late = after([symmetric, branch_late], grad_pre[0], *qkv_sum.sent, feed_sum.given)
    memory_sum = GroupSum(plane, [(normed, *grad_pre)])
    ffn_sum.sent = after(ffn_sum.sent, *memory_sum.sent)
    ffn_sum.cores()
    ffn_own = ffn_sum.chips()
    block_out = turn(absolute((middle + ffn_own).astype(BF16)))
    qkv_sum.line()
    out_grad_sum.cores(memory_sum.sent)
    grad_pre_late = after(grad_pre, *memory_sum.sent, *qkv_sum.sent)
    normed_sum = RowSum(
        dot(mixing, branch, 0, 0)
        + sum_dots(
            first_layer,
            [(grad_pre_late[i], i, 0, units, 1) for i in both] + [(grad_qkv[i], i, units, q_end, 0) for i in both],
        ).astype(F32)
    )
    normed_sum.cores()
    memory_sum.second([normed_sum.sent, out_grad_sum.given])
    qkv_sum.cores(memory_sum.sent)

    grad_table = after(grad_table, *memory_sum.sent)
    for axis in ("c", "l"):
        grad_table = grad_table + swap(grad_table, axis)
    grad_alpha, grad_eta = span_table_back(kept_table, grad_table)
    grad_logits = jnp.stack([grad_alpha * alpha * (1.0 - alpha), grad_eta * eta * (1.0 - eta)]) / CH
    grad_vectors = jnp.sum(grad_logits[:, :, None] * span_sums[None], axis=1)
    own_logits = lax.dynamic_slice_in_dim(grad_logits, member * own_spans, own_spans, 1)
    grad_spans = jnp.sum(own_logits[:, :, None] * gates[:, None, :], axis=0)
    grad_normed = after(normed_sum.chips(), *memory_sum.sent) + jnp.repeat(grad_spans, CH, axis=0)
    back_one, grad_gain_one = norm_back(x_own, inverse_one, gain_one, grad_normed)
    grad_block_in = turn(absolute((grad_middle + back_one).astype(BF16))).astype(F32)

    memory_sum.line()
    memory_sum.cores([grad_gain_one])
    grad_gate, grad_up, grad_down = feed_sum.results()
    (grad_qkv_sum,) = qkv_sum.results()
    grad_memory_out, grad_project_out = out_grad_sum.results()
    (grad_memory_in,) = memory_sum.results()

    gram = 0.0
    for i in both:
        blocks = act[i].reshape(spans, CH, -1)
        gram = gram + jnp.einsum("cth,csh->cts", blocks, blocks, preferred_element_type=F32)
    written = (normed * valid[:, None].astype(BF16)).reshape(spans, CH, width)
    cross = jnp.einsum("ctd,csd->cts", written, written, preferred_element_type=F32)
    piece = jnp.sum(gram * cross, axis=(1, 2))
    piece = after(piece, *memory_sum.sent)
    for axis in ("c", "l"):
        piece = piece + swap(piece, axis)
    surprise = jnp.sqrt(piece / (hidden_units * width * CH))
    weight = jnp.sum(valid.reshape(spans, CH), axis=1)
    numbers = jnp.stack(
        [jnp.sum(weight * surprise), jnp.sum(weight * alpha), jnp.sum(weight * eta), jnp.sum(weight)]
    )
    small = jnp.stack([grad_gain_one, grad_vectors[0] * 0.25, grad_vectors[1] * 0.25, grad_gain_two])
    small = cat([absolute(small), jnp.pad(numbers[None], ((0, 0), (0, width - 4)))], 0)
    small = all_sum(plane, small)
    logged = small[4, :3] / small[4, 3]
    share = gain_in.shape[0]
    index = lax.axis_index(plane + ("c", "h", "l"))
    mine = lax.dynamic_slice_in_dim(small, index * share, share, 1)
    grad_project_in = jnp.stack(
        [
            cat([grad_qkv_sum[:, (3 * j + i) * q_cols : (3 * j + i + 1) * q_cols] for j in both], 1)
            for i in range(3)
        ]
    )
    return (
        block_out,
        grad_block_in,
        mine[0],
        mine[1],
        mine[2],
        grad_project_in,
        grad_project_out.T,
        grad_memory_in,
        grad_memory_out.T,
        mine[3],
        grad_gate,
        grad_up,
        grad_down.T,
        logged,
    )


def solution(mesh):
    chips, line = mesh.shape["dp"] // 2, mesh.shape["mp"]
    if chips == 4:
        plane, sizes = ("y", "x"), (2, 2)
    else:
        plane, sizes = ("p",), (chips,)
    fine = Mesh(mesh.devices.reshape(sizes + (2, line // 2, 2)), plane + ("c", "h", "l"))
    dp, mp = plane + ("c",), ("h", "l")
    every = dp + mp
    placed = (
        P(every, None),
        P(every, None),
        P(dp, None),
        P(dp),
        P(every),
        P(every),
        P(every),
        P(None, dp, mp),
        P(mp, dp),
        P(dp, mp),
        P(mp, dp),
        P(every),
        P(dp, mp),
        P(dp, mp),
        P(mp, dp),
    )
    return jax.shard_map(
        functools.partial(on_device, plane),
        mesh=fine,
        in_specs=placed,
        out_specs=(
            P(every, None),
            P(every, None),
            P(every),
            P(every),
            P(every),
            P(None, dp, mp),
            P(mp, dp),
            P(dp, mp),
            P(mp, dp),
            P(every),
            P(dp, mp),
            P(dp, mp),
            P(mp, dp),
            P(),
        ),
        check_vma=False,
    )
```

```python
import functools

import jax
import jax.numpy as jnp
from jax import lax
from jax.experimental import pallas as pl
from jax.experimental.layout import Layout, with_layout_constraint
from jax.experimental.pallas import tpu as pltpu
from jax.sharding import Mesh
from jax.sharding import PartitionSpec as P

HD = 96
CH = 64
EPS = 1e-06
ALPHA_SHIFT = 1.5
ETA_SHIFT = 0.5
NEG = -1e30
SCALE = HD ** (-0.5)
F32 = jnp.float32
BF16 = jnp.bfloat16
VMEM_LIMIT = 24 * 1024 * 1024

def dot(a, b, ca, cb):
    return lax.dot_general(a, b, (((ca,), (cb,)), ((), ())), preferred_element_type=F32)


def swap(x, axis):
    return lax.ppermute(x, axis, [(0, 1), (1, 0)])


def turn(x):
    return lax.ppermute(x, ("c", "h"), [(0, 0), (1, 2), (2, 1), (3, 3)])


def after(x, *others):
    if isinstance(x, (list, tuple)):
        return list(lax.optimization_barrier((*x, *others))[: len(x)])
    return lax.optimization_barrier((x, *others))[0]


def cat(parts, axis=0):
    return jnp.concatenate(parts, axis=axis)


def by_rows(x):
    return with_layout_constraint(x, Layout(major_to_minor=tuple(range(x.ndim))))


def by_index(index, first, second, axis=0):
    return cat([jnp.where(index == 0, first, second), jnp.where(index == 0, second, first)], axis)


def gather_rows(x):
    c, l = lax.axis_index("c"), lax.axis_index("l")
    half = by_index(l, x, swap(x, "l"))
    return by_index(c, half, swap(half, "c"))


class RowSum:
    def __init__(self, x):
        c = lax.axis_index("c")
        rows = x.shape[0] // 2
        self.sent = lax.dynamic_slice_in_dim(x, (1 - c) * rows, rows, 0).astype(BF16)
        self.kept = lax.dynamic_slice_in_dim(x, c * rows, rows, 0)

    def cores(self):
        l = lax.axis_index("l")
        half = self.kept.astype(F32) + swap(self.sent, "c").astype(F32)
        rows = half.shape[0] // 2
        self.sent = lax.dynamic_slice_in_dim(half, (1 - l) * rows, rows, 0).astype(BF16)
        self.kept = lax.dynamic_slice_in_dim(half, l * rows, rows, 0)

    def chips(self):
        return self.kept + swap(self.sent, "l").astype(F32)


def shuffle(plane, v, back=False):
    if len(plane) == 1:
        return v
    share = v.shape[-1] // 4
    b = [v[..., i * share : (i + 1) * share] for i in range(4)]
    if back:
        b = [b[0], b[1], b[3], b[2]]
    x, y = lax.axis_index("x"), lax.axis_index("y")
    b = [jnp.where(x == 0, b[i], b[i ^ 1]) for i in range(4)]
    b = [jnp.where(y == 0, b[i], b[i ^ 2]) for i in range(4)]
    if not back:
        b = [b[0], b[1], b[3], b[2]]
    return cat(b, -1)


class PlaneGather:
    def __init__(self, plane, piece, first):
        if len(plane) == 1:
            self.parts = [lax.all_gather(piece, plane, axis=0, tiled=True)]
            self.near, self.far = self.parts, self.parts[0]
            return
        near = {axis: swap(piece, axis) for axis in plane}
        second = "y" if first == "x" else "x"
        self.far = swap(near[first], second)
        self.near = [near["x"], near["y"]]
        self.parts = [piece, near["x"], self.far, near["y"]]

    def whole(self):
        return by_rows(cat(self.parts) if len(self.parts) > 1 else self.parts[0])


class PlaneSum:
    def __init__(self, plane, pairs, first):
        self.plane, self.pairs, self.first = plane, pairs, first
        width = pairs[0][0].shape[1]
        self.w = w = width // 4
        if len(plane) == 1:
            self.sent = self.product(0, width)
        elif first == "x":
            self.sent = self.product(w, 3 * w)
        else:
            self.sent = self.product(2 * w, 4 * w)

    def product(self, start, stop):
        parts = [dot(left[:, start:stop], right, 0, 0).astype(BF16) for left, right in self.pairs]
        return cat(parts, 1) if len(parts) > 1 else parts[0]

    def second(self, ties=()):
        if len(self.plane) == 1:
            self.total = lax.psum_scatter(self.sent, self.plane, scatter_dimension=0, tiled=True).astype(F32)
            self.sent = self.got = self.total
            return
        w = self.w
        self.got = got = after(swap(self.sent, self.first), *ties)
        if self.first == "x":
            self.axis, mine, other, other_at = "y", got[:w], got[w:], 3
        else:
            self.axis, mine, other, other_at = "x", got[w:], got[:w], 1
        other = self.product(other_at * w, (other_at + 1) * w).astype(F32) + other.astype(F32)
        self.sent = other.astype(BF16)
        self.total = self.product(0, w).astype(F32) + mine.astype(F32)

    def last(self):
        if len(self.plane) > 1:
            self.total = self.total + swap(self.sent, self.axis).astype(F32)


class GroupSum:
    def __init__(self, plane, sources):
        self.columns = [right.shape[1] for _, right, _ in sources]
        self.here = PlaneSum(plane, [(left, right) for left, right, _ in sources], "x")
        self.there = PlaneSum(plane, [(left, right) for left, _, right in sources], "y")
        self.sent = [self.here.sent, self.there.sent]

    def second(self, ties=()):
        self.here.second(ties)
        self.there.second(ties)
        self.sent = [self.here.sent, self.there.sent]

    def line(self):
        self.there.last()
        self.sent = [self.there.total.astype(BF16)]
        self.here.last()
        self.sent.append(self.here.total)

    def cores(self, ties=()):
        got = swap(self.sent[0], "h")
        mine = self.here.total + (after(got, *ties) if ties else got).astype(F32)
        c = lax.axis_index("c")
        rows = mine.shape[0] // 2
        self.given = lax.dynamic_slice_in_dim(mine, (1 - c) * rows, rows, 0).astype(BF16)
        self.kept = lax.dynamic_slice_in_dim(mine, c * rows, rows, 0)

    def results(self):
        c = lax.axis_index("c")
        got = swap(self.given, "c").astype(F32)
        results, start = [], 0
        for n in self.columns:
            results.append(by_index(c, self.kept[:, start : start + n], got[:, start : start + n], 1))
            start += n
        return results


def pack(groups, common=()):
    c = lax.axis_index("c")
    mine, other, results, start = [], [], [], 0
    for shards in groups:
        columns = sum(s.shape[1] // 2 for s in shards) + sum(s.shape[1] for s in common)
        filled = list(common)
        if columns % 128:
            filled.append(jnp.zeros((shards[0].shape[0], 128 - columns % 128), BF16))
        low = cat([s[:, : s.shape[1] // 2] for s in shards] + filled, 1)
        high = cat([s[:, s.shape[1] // 2 :] for s in shards] + filled, 1)
        mine.append(jnp.where(c == 0, low, high))
        other.append(jnp.where(c == 0, high, low))
    got = swap(cat(other, 1), "c")
    for block in mine:
        results.append(by_rows(by_index(c, block, got[:, start : start + block.shape[1]])))
        start += block.shape[1]
    return results


def tall(x):
    padding = 128 - x.shape[0]
    wide = cat([x.astype(F32), jnp.zeros((padding, x.shape[1]), F32)])
    return wide.astype(BF16), wide.T.astype(BF16)


def attend_kernel(code_ref, doc_ref, qkv_ref, ctx_ref, lse_ref, bias_ref):
    length = qkv_ref.shape[-1]
    heads = qkv_ref.shape[0] // (3 * HD)
    block = min(256, length)
    fill_bias(code_ref, doc_ref, bias_ref)
    for head in range(heads):
        part = [slice((i * heads + head) * HD, (i * heads + head + 1) * HD) for i in range(3)]
        v = qkv_ref[part[2]]
        q, _ = tall(qkv_ref[part[0]])
        _, k = tall(qkv_ref[part[1]])
        for start in range(0, length, block):
            end = start + block
            cols = slice(start, end)
            s = dot(k[:end], q[:, cols], 1, 0) * SCALE + bias_ref[:end, cols]
            top = jnp.max(s, axis=0, keepdims=True)
            e = jnp.exp(s - top)
            total = jnp.sum(e, axis=0, keepdims=True)
            p = (e * (1.0 / total)).astype(BF16)
            ctx_ref[part[0], cols] = dot(v[:, :end], p, 1, 0).astype(BF16)
            lse_ref[head : head + 1, cols] = top + jnp.log(total)


def sum_kernel(terms, weights, *refs):
    weight_refs, left_refs, out_ref = refs[:weights], refs[weights:-1], refs[-1]
    total = None
    for (which, start, stop, side), left_ref in zip(terms, left_refs):
        right = weight_refs[which][:, start:stop]
        part = dot(left_ref[...], right, side, 1)
        total = part if total is None else total + part
    out_ref[...] = total.astype(BF16)


def sum_dots(weights, terms):
    left, side = terms[0][0], terms[0][4]
    rows, width = left.shape[1 - side], weights[0].shape[0]
    tile, wide = min(512, rows), 512
    in_specs = [pl.BlockSpec((wide, w.shape[1]), lambda n, m: (n, 0)) for w in weights]
    for left, _, _, _, side in terms:
        if side == 1:
            in_specs.append(pl.BlockSpec((tile, left.shape[1]), lambda n, m: (m, 0)))
        else:
            in_specs.append(pl.BlockSpec((left.shape[0], tile), lambda n, m: (0, m)))
    return pl.pallas_call(
        functools.partial(sum_kernel, [t[1:] for t in terms], len(weights)),
        grid=(width // wide, rows // tile),
        in_specs=in_specs,
        out_specs=pl.BlockSpec((tile, wide), lambda n, m: (m, n)),
        out_shape=jax.ShapeDtypeStruct((rows, width), BF16),
        compiler_params=pltpu.CompilerParams(vmem_limit_bytes=VMEM_LIMIT),
        cost_estimate=pl.CostEstimate(
            flops=2 * rows * width * sum(t[3] - t[2] for t in terms),
            bytes_accessed=2 * sum(w.size for w in weights) + 8 * sum(t[0].size for t in terms),
            transcendentals=0,
        ),
    )(*weights, *[t[0] for t in terms])


def fill_bias(code_ref, doc_ref, bias_ref):
    length = bias_ref.shape[0]
    block = min(256, length)
    for start in range(0, length, block):
        u = start + lax.broadcasted_iota(jnp.int32, (block, length), 0)
        t = lax.broadcasted_iota(jnp.int32, (block, length), 1)
        same = code_ref[start : start + block, :] == doc_ref[...]
        allow = ((u <= t) & same) | (u == t)
        bias_ref[start : start + block, :] = jnp.where(allow, 0.0, NEG)


def attend_back_kernel(code_ref, doc_ref, qkv_ref, lse_ref, grad_ref, out_ref, bias_ref, acc_ref):
    length = qkv_ref.shape[-1]
    heads = qkv_ref.shape[0] // (3 * HD)
    block = min(256, length)
    fill_bias(code_ref, doc_ref, bias_ref)
    for head in range(heads):
        part = [slice((i * heads + head) * HD, (i * heads + head + 1) * HD) for i in range(3)]
        q, kt, g = qkv_ref[part[0]], qkv_ref[part[1]], grad_ref[part[0]]
        q_wide, _ = tall(q)
        g_wide, _ = tall(g)
        _, k = tall(kt)
        _, v = tall(qkv_ref[part[2]])
        acc_ref[...] = jnp.zeros_like(acc_ref)
        for start in range(0, length, block):
            end = start + block
            cols = slice(start, end)
            s = dot(k[:end], q_wide[:, cols], 1, 0) * SCALE + bias_ref[:end, cols]
            p = jnp.exp(s - lse_ref[head : head + 1, cols])
            dp = dot(v[:end], g_wide[:, cols], 1, 0)
            inner = jnp.sum(p * dp, axis=0, keepdims=True)
            ds = (p * (dp - inner)).astype(BF16)
            out_ref[part[0], cols] = (dot(kt[:, :end], ds, 1, 0) * SCALE).astype(BF16)
            acc_ref[0, :, :end] += dot(q[:, cols], ds, 1, 1)
            acc_ref[1, :, :end] += dot(g[:, cols], p.astype(BF16), 1, 1)
        out_ref[part[1]] = (acc_ref[0] * SCALE).astype(BF16)
        out_ref[part[2]] = acc_ref[1].astype(BF16)


def attend(code, doc, qkv):
    heads, length = qkv.shape[0] // (3 * HD), qkv.shape[1]
    return pl.pallas_call(
        attend_kernel,
        out_shape=[
            jax.ShapeDtypeStruct((heads * HD, length), BF16),
            jax.ShapeDtypeStruct((heads, length), F32),
        ],
        scratch_shapes=[pltpu.VMEM((length, length), F32)],
        compiler_params=pltpu.CompilerParams(vmem_limit_bytes=VMEM_LIMIT),
        cost_estimate=pl.CostEstimate(
            flops=heads * length * length * HD * 4,
            bytes_accessed=heads * HD * length * 8,
            transcendentals=heads * length * length,
        ),
    )(code, doc, qkv)


def attend_back(code, doc, qkv, lse, grad):
    heads, length = qkv.shape[0] // (3 * HD), qkv.shape[1]
    return pl.pallas_call(
        attend_back_kernel,
        out_shape=jax.ShapeDtypeStruct(qkv.shape, BF16),
        scratch_shapes=[pltpu.VMEM((length, length), F32), pltpu.VMEM((2, HD, length), F32)],
        compiler_params=pltpu.CompilerParams(vmem_limit_bytes=VMEM_LIMIT),
        cost_estimate=pl.CostEstimate(
            flops=heads * length * length * HD * 10,
            bytes_accessed=heads * HD * length * 14,
            transcendentals=heads * length * length,
        ),
    )(code, doc, qkv, lse, grad)


def table_kernel(alpha_ref, eta_ref, keep_ref, table_ref, state_ref):
    spans = table_ref.shape[0]
    place = lax.broadcasted_iota(jnp.int32, (1, table_ref.shape[1]), 1)
    state = jnp.zeros((1, table_ref.shape[1]), F32)
    memory = jnp.zeros((1, table_ref.shape[1]), F32)
    for c in range(spans):
        kept = keep_ref[c : c + 1, :]
        table_ref[c : c + 1, :] = memory * kept
        state_ref[c : c + 1, :] = state * kept
        state = eta_ref[c : c + 1, :] * kept * state + jnp.where(place == c, 1.0, 0.0)
        memory = alpha_ref[c : c + 1, :] * kept * memory + state


def table_back_kernel(alpha_ref, eta_ref, keep_ref, table_ref, state_ref, grad_ref, out_ref, ga_ref, ge_ref):
    spans = table_ref.shape[0]
    wide = (1, table_ref.shape[1])
    grad_state = jnp.zeros(wide, F32)
    grad_memory = jnp.zeros(wide, F32)
    for c in reversed(range(spans)):
        kept = keep_ref[c : c + 1, :]
        grad_state = grad_state + grad_memory
        ga_ref[c : c + 1, :] = grad_memory * table_ref[c : c + 1, :]
        ge_ref[c : c + 1, :] = grad_state * state_ref[c : c + 1, :]
        grad_state = eta_ref[c : c + 1, :] * kept * grad_state
        grad_memory = kept * (alpha_ref[c : c + 1, :] * grad_memory + grad_ref[c : c + 1, :])
    out_ref[0] = jnp.broadcast_to(jnp.sum(ga_ref[...], axis=1, keepdims=True), out_ref.shape[1:])
    out_ref[1] = jnp.broadcast_to(jnp.sum(ge_ref[...], axis=1, keepdims=True), out_ref.shape[1:])


def span_table(alpha, eta, keep):
    spans = alpha.shape[0]
    wide = lambda v: jnp.broadcast_to(v[:, None], (spans, 128))
    square = jax.ShapeDtypeStruct((spans, 128), F32)
    args = (wide(alpha), wide(eta), wide(keep))
    table, state = pl.pallas_call(table_kernel, out_shape=[square, square])(*args)
    return table, (args, table, state)


def span_table_back(kept, grad):
    args, table, state = kept
    spans = table.shape[0]
    scratch = pltpu.VMEM((spans, 128), F32)
    grad = jnp.pad(grad, ((0, 0), (0, 128 - grad.shape[1])))
    both = pl.pallas_call(
        table_back_kernel,
        out_shape=jax.ShapeDtypeStruct((2, spans, 128), F32),
        scratch_shapes=[scratch, scratch],
    )(*args, table, state, grad)
    return both[0, :, 0], both[1, :, 0]


def norm_back(values, inverse, gain, grad):
    scaled = grad * gain
    inner = jnp.mean(values * scaled, axis=-1, keepdims=True)
    grad_values = inverse * scaled - values * inverse * inverse * inverse * inner
    grad_gain = jnp.sum(grad * values * inverse, axis=0)
    return grad_values, grad_gain


def inverse_of(values):
    return lax.rsqrt(jnp.mean(values * values, axis=-1, keepdims=True) + EPS)


def all_sum(plane, v):
    for axis in ("l", "h", "c"):
        v = v + swap(v, axis)
    if len(plane) == 1:
        return lax.psum(v, plane)
    for axis in ("x", "y"):
        v = v + swap(v, axis)
    return v


def all_parts(plane, v):
    for axis in ("l", "h", "c"):
        v = by_index(lax.axis_index(axis), v, swap(v, axis))
    if len(plane) == 1:
        return lax.all_gather(v, plane, axis=0, tiled=True)
    for axis in ("x", "y"):
        v = by_index(lax.axis_index(axis), v, swap(v, axis))
    return v


def on_device(
    plane,
    block_in,
    grad_out,
    resets,
    counts,
    gain_in,
    w_forget,
    w_momentum,
    project_in,
    project_out,
    memory_in,
    memory_out,
    gain_mid,
    gate_weight,
    up_weight,
    down_weight,
):
    relative = functools.partial(shuffle, plane)
    absolute = functools.partial(shuffle, plane, back=True)
    c, l = lax.axis_index("c"), lax.axis_index("l")
    quarter, width = block_in.shape
    length = 4 * quarter
    spans = length // CH
    own_spans = quarter // CH
    member = 2 * c + l
    hidden_units = 4 * memory_in.shape[1]
    units, q_cols, ff = memory_in.shape[1] // 2, project_in.shape[2] // 2, gate_weight.shape[1] // 2

    vectors = cat([v[None] for v in (gain_in, w_forget, w_momentum, gain_mid)], 0)
    for axis in ("l", "h"):
        vectors = by_index(lax.axis_index(axis), vectors, swap(vectors, axis), 1)
    first = [memory_in, project_in[0], project_in[1], project_in[2]]
    x_turned = turn(block_in)
    flags = turn(cat([resets, counts[:, None]], 1))
    (share0,) = pack([first], [vectors.T])
    far0 = swap(after(share0, x_turned), "h")
    late = after([memory_out.T, project_out.T, gate_weight, up_weight, down_weight.T], share0)
    share1, share2 = pack([late[:2], late[2:]])
    x_own = relative(x_turned)
    half = by_index(l, x_own, swap(x_own, "l"))
    other_half = swap(half, "c")
    x_full = by_index(c, half, other_half)
    stages = [PlaneGather(plane, share0, "x")]
    share1 = after(share1, *stages[0].near)
    stages.append(PlaneGather(plane, share1, "y"))
    far0 = after(far0, *stages[0].near)
    stages.append(PlaneGather(plane, far0, "x"))
    far1 = swap(after(share1, far0), "h")
    first_here = stages[0].whole()
    both = range(2)
    q_end = units + 3 * q_cols
    out_end = units + q_cols
    vectors = first_here[:, q_end : q_end + 4].T.astype(F32)
    gain_one, gain_two, gates = vectors[0], vectors[3], vectors[1:3]

    x_wide = x_full.astype(F32)
    normed = (x_wide * inverse_of(x_wide) * gain_one).astype(BF16)

    act, slope_pre, qkv, ctx, lse = [], [], [], [], []

    def memory(first):
        pre = dot(normed, first[:, :units], 1, 0)
        sig_pre = jax.nn.sigmoid(pre)
        act.append((pre * sig_pre).astype(BF16))
        slope_pre.append((sig_pre * (1.0 + pre * (1.0 - sig_pre))).astype(BF16))

    memory(first_here)
    far1 = after(far1, *stages[2].near, *stages[1].near, stages[2].far, act[0])
    stages.append(PlaneGather(plane, far1, "y"))
    far2 = swap(after(share2, far1), "h")
    share2 = after(share2, *stages[3].near, stages[1].far, stages[2].far, stages[3].far)
    stages.append(PlaneGather(plane, share2, "x"))
    grad_turned = turn(after(grad_out, far2))
    far2 = after(far2, *stages[4].near, stages[3].far)
    stages.append(PlaneGather(plane, far2, "y"))
    first_layer, second_layer, feed = (
        [first_here, stages[2].whole()],
        [stages[1].whole(), stages[3].whole()],
        [stages[4].whole(), stages[5].whole()],
    )

    resets, count = flags[0, :-1], flags[0, -1]
    positions = jnp.arange(length, dtype=jnp.int32)
    valid = (positions < count).astype(F32)
    keep = (1 - resets).astype(F32)
    doc = jnp.repeat(jnp.cumsum(resets, dtype=jnp.int32), CH).astype(F32)
    code = jnp.where(valid > 0, doc, -1.0)[:, None]
    doc = doc[None, :]

    x_own = x_own.astype(F32)
    inverse_one = inverse_of(x_own)
    span_sums = jnp.sum(normed.reshape(spans, CH, width).astype(F32), axis=1)
    logits = jnp.sum(span_sums[None] * gates[:, None, :], axis=2) / CH
    alpha = jax.nn.sigmoid(logits[0] + ALPHA_SHIFT)
    eta = jax.nn.sigmoid(logits[1] + ETA_SHIFT)
    table, kept_table = span_table(alpha, eta, keep)

    memory(first_layer[1])
    for i in both:
        qkv.append(dot(first_layer[i][:, units:q_end], normed, 0, 1).astype(BF16))
    sim_sum = RowSum((dot(act[0], act[0], 1, 1) + dot(act[1], act[1], 1, 1)) / hidden_units)
    sim_sum.cores()
    sim = sim_sum.chips()
    qkv[1] = after(qkv[1], *stages[4].near)
    for i in both:
        context, logsum = attend(code, doc, qkv[i])
        ctx.append(context)
        lse.append(logsum)
    out_sum = RowSum(
        sum_dots(
            second_layer,
            [(act[i], i, 0, units, 1) for i in both] + [(ctx[i], i, units, out_end, 0) for i in both],
        )
    )
    out_sum.cores()
    out_own = out_sum.chips()
    table_own = lax.dynamic_slice_in_dim(table[:, :spans], member * own_spans, own_spans, 0)
    spread = jnp.repeat(jnp.repeat(table_own, CH, axis=0), CH, axis=1)
    sim = after(sim, *stages[5].near)
    mixing = (sim * spread * valid[None, :] / CH).astype(BF16)
    middle = x_own + out_own + dot(mixing, normed, 1, 0)
    inverse_two = inverse_of(middle)
    mid = (middle * inverse_two * gain_two).astype(BF16)
    mid_all = gather_rows(mid)
    grad_own = relative(grad_turned)
    grad_all = gather_rows(grad_own)

    hidden, grad_gate_pre, grad_up_pre = [], [], []
    for i in both:
        gate = dot(mid_all, feed[i][:, :ff], 1, 0)
        up = dot(mid_all, feed[i][:, ff : 2 * ff], 1, 0)
        grad_hidden = dot(grad_all, feed[i][:, 2 * ff :], 1, 0)
        sigma = jax.nn.sigmoid(gate)
        swish = gate * sigma
        hidden.append((swish * up).astype(BF16))
        grad_gate_pre.append((grad_hidden * up * (sigma * (1.0 + gate * (1.0 - sigma)))).astype(BF16))
        grad_up_pre.append((grad_hidden * swish).astype(BF16))
    mid_sum = RowSum(
        sum_dots(
            feed,
            [(grad_gate_pre[i], i, 0, ff, 1) for i in both] + [(grad_up_pre[i], i, ff, 2 * ff, 1) for i in both],
        )
    )
    mid_sum.cores()
    mid_late, grad_late = after([mid_all, grad_all], mid_sum.sent)
    feed_sum = GroupSum(
        plane, [(mid_late, *grad_gate_pre), (mid_late, *grad_up_pre), (grad_late, *hidden)]
    )
    hidden = after(hidden, mid_sum.sent, *feed_sum.sent)
    ffn_sum = RowSum(sum_dots(feed, [(hidden[i], i, 2 * ff, 3 * ff, 1) for i in both]))
    grad_mid = after(mid_sum.chips(), ffn_sum.sent)

    back_two, grad_gain_two = norm_back(middle, inverse_two, gain_two, grad_mid)
    grad_middle = grad_own.astype(F32) + back_two
    branch = grad_middle.astype(BF16)
    branch_all = gather_rows(branch)
    scaled = dot(branch, normed, 1, 1) / CH * valid[None, :]
    grad_sim_own = (scaled * spread).astype(BF16)
    grad_sim = gather_rows(grad_sim_own)
    grad_blocks = jnp.sum((scaled * sim).reshape(own_spans, CH, spans, CH), axis=(1, 3))
    grad_table = lax.dynamic_update_slice_in_dim(
        jnp.zeros((spans, spans), F32), grad_blocks, member * own_spans, 0
    )

    feed_sum.second()
    branch_all = after(branch_all, *feed_sum.sent)
    out_grad_sum = GroupSum(plane, [(branch_all, *act), (branch_all, ctx[0].T, ctx[1].T)])
    ffn_sum.sent = after(ffn_sum.sent, branch_all)
    ffn_sum.cores()
    branch_all = after(branch_all, *out_grad_sum.sent, ffn_sum.sent)
    grad_pre, grad_qkv = [], []
    for i in both:
        grad_ctx = dot(second_layer[i][:, units:out_end], branch_all, 0, 1).astype(BF16)
        grad_qkv.append(attend_back(code, doc, qkv[i], lse[i], grad_ctx))
    feed_sum.line()
    out_grad_sum.second()
    normed_late = after(normed, *feed_sum.sent, *grad_qkv, *out_grad_sum.sent)
    qkv_sum = GroupSum(plane, [(normed_late, grad_qkv[0].T, grad_qkv[1].T)])
    out_grad_sum.line()
    grad_sim, branch_late = after([grad_sim, branch_all], *qkv_sum.sent, *out_grad_sum.sent)
    symmetric = (grad_sim.astype(F32) + grad_sim.T.astype(F32)).astype(BF16)
    for i in both:
        grad_act = (
            dot(branch_late, second_layer[i][:, :units], 1, 0) + dot(symmetric, act[i], 1, 0) / hidden_units
        )
        grad_pre.append((grad_act * slope_pre[i].astype(F32)).astype(BF16))
        if i == 0:
            qkv_sum.second()
            feed_sum.cores([grad_pre[0]])
            symmetric, branch_late = after([symmetric, branch_late], grad_pre[0], *qkv_sum.sent, feed_sum.given)
    memory_sum = GroupSum(plane, [(normed, *grad_pre)])
    ffn_sum.sent = after(ffn_sum.sent, *memory_sum.sent)
    block_out = turn(absolute((middle + ffn_sum.chips()).astype(BF16)))
    qkv_sum.line()
    out_grad_sum.cores(memory_sum.sent)
    grad_pre_late = after(grad_pre, *memory_sum.sent, *qkv_sum.sent)
    normed_sum = RowSum(
        dot(mixing, branch, 0, 0)
        + sum_dots(
            first_layer,
            [(grad_pre_late[i], i, 0, units, 1) for i in both] + [(grad_qkv[i], i, units, q_end, 0) for i in both],
        ).astype(F32)
    )
    normed_sum.cores()
    memory_sum.second([normed_sum.sent, out_grad_sum.given])
    qkv_sum.cores(memory_sum.sent)

    grad_table = after(grad_table, *memory_sum.sent)
    for axis in ("c", "l"):
        grad_table = grad_table + swap(grad_table, axis)
    grad_alpha, grad_eta = span_table_back(kept_table, grad_table)
    grad_logits = jnp.stack([grad_alpha * alpha * (1.0 - alpha), grad_eta * eta * (1.0 - eta)]) / CH
    grad_vectors = jnp.sum(grad_logits[:, :, None] * span_sums[None], axis=1)
    own_logits = lax.dynamic_slice_in_dim(grad_logits, member * own_spans, own_spans, 1)
    grad_spans = jnp.sum(own_logits[:, :, None] * gates[:, None, :], axis=0)
    grad_normed = after(normed_sum.chips(), *memory_sum.sent, block_out) + jnp.repeat(grad_spans, CH, axis=0)
    back_one, grad_gain_one = norm_back(x_own, inverse_one, gain_one, grad_normed)
    grad_block_in = turn(absolute((grad_middle + back_one).astype(BF16))).astype(F32)

    memory_sum.line()
    memory_sum.cores([grad_gain_one])
    grad_gate, grad_up, grad_down = feed_sum.results()
    (grad_qkv_sum,) = qkv_sum.results()
    grad_memory_out, grad_project_out = out_grad_sum.results()
    (grad_memory_in,) = memory_sum.results()

    gram = 0.0
    for i in both:
        blocks = act[i].reshape(spans, CH, -1)
        gram = gram + jnp.einsum("cth,csh->cts", blocks, blocks, preferred_element_type=F32)
    written = (normed * valid[:, None].astype(BF16)).reshape(spans, CH, width)
    cross = jnp.einsum("ctd,csd->cts", written, written, preferred_element_type=F32)
    piece = jnp.sum(gram * cross, axis=(1, 2))
    piece = after(piece, *memory_sum.sent)
    for axis in ("c", "l"):
        piece = piece + swap(piece, axis)
    surprise = jnp.sqrt(piece / (hidden_units * width * CH))
    weight = jnp.sum(valid.reshape(spans, CH), axis=1)
    numbers = jnp.stack(
        [jnp.sum(weight * surprise), jnp.sum(weight * alpha), jnp.sum(weight * eta), jnp.sum(weight)]
    )
    small = jnp.stack([grad_gain_one, grad_vectors[0] * 0.25, grad_vectors[1] * 0.25, grad_gain_two])
    small = cat([absolute(small), jnp.pad(numbers[None], ((0, 0), (0, width - 4)))], 0)
    small = all_sum(plane, small)
    logged = small[4, :3] / small[4, 3]
    share = gain_in.shape[0]
    index = lax.axis_index(plane + ("c", "h", "l"))
    mine = lax.dynamic_slice_in_dim(small, index * share, share, 1)
    grad_project_in = jnp.stack(
        [
            cat([grad_qkv_sum[:, (3 * j + i) * q_cols : (3 * j + i + 1) * q_cols] for j in both], 1)
            for i in range(3)
        ]
    )
    return (
        block_out,
        grad_block_in,
        mine[0],
        mine[1],
        mine[2],
        grad_project_in,
        grad_project_out.T,
        grad_memory_in,
        grad_memory_out.T,
        mine[3],
        grad_gate,
        grad_up,
        grad_down.T,
        logged,
    )


def solution(mesh):
    chips, line = mesh.shape["dp"] // 2, mesh.shape["mp"]
    if chips == 4:
        plane, sizes = ("y", "x"), (2, 2)
    else:
        plane, sizes = ("p",), (chips,)
    fine = Mesh(mesh.devices.reshape(sizes + (2, line // 2, 2)), plane + ("c", "h", "l"))
    dp, mp = plane + ("c",), ("h", "l")
    every = dp + mp
    placed = (
        P(every, None),
        P(every, None),
        P(dp, None),
        P(dp),
        P(every),
        P(every),
        P(every),
        P(None, dp, mp),
        P(mp, dp),
        P(dp, mp),
        P(mp, dp),
        P(every),
        P(dp, mp),
        P(dp, mp),
        P(mp, dp),
    )
    return jax.shard_map(
        functools.partial(on_device, plane),
        mesh=fine,
        in_specs=placed,
        out_specs=(
            P(every, None),
            P(every, None),
            P(every),
            P(every),
            P(every),
            P(None, dp, mp),
            P(mp, dp),
            P(dp, mp),
            P(mp, dp),
            P(every),
            P(dp, mp),
            P(dp, mp),
            P(mp, dp),
            P(),
        ),
        check_vma=False,
    )
```

```python
import functools

import jax
import jax.numpy as jnp
from jax import lax
from jax.experimental import pallas as pl
from jax.experimental.layout import Layout, with_layout_constraint
from jax.experimental.pallas import tpu as pltpu
from jax.sharding import Mesh
from jax.sharding import PartitionSpec as P

HD = 96
CH = 64
EPS = 1e-06
ALPHA_SHIFT = 1.5
ETA_SHIFT = 0.5
NEG = -1e30
SCALE = HD ** (-0.5)
F32 = jnp.float32
BF16 = jnp.bfloat16
VMEM_LIMIT = 24 * 1024 * 1024

def dot(a, b, ca, cb):
    return lax.dot_general(a, b, (((ca,), (cb,)), ((), ())), preferred_element_type=F32)


def swap(x, axis):
    return lax.ppermute(x, axis, [(0, 1), (1, 0)])


def turn(x):
    return lax.ppermute(x, ("c", "h"), [(0, 0), (1, 2), (2, 1), (3, 3)])


def after(x, *others):
    if isinstance(x, (list, tuple)):
        return list(lax.optimization_barrier((*x, *others))[: len(x)])
    return lax.optimization_barrier((x, *others))[0]


def cat(parts, axis=0):
    return jnp.concatenate(parts, axis=axis)


def by_rows(x):
    return with_layout_constraint(x, Layout(major_to_minor=tuple(range(x.ndim))))


def by_index(index, first, second, axis=0):
    return cat([jnp.where(index == 0, first, second), jnp.where(index == 0, second, first)], axis)


def gather_rows(x):
    c, l = lax.axis_index("c"), lax.axis_index("l")
    half = by_index(l, x, swap(x, "l"))
    return by_index(c, half, swap(half, "c"))


class RowSum:
    def __init__(self, x):
        c = lax.axis_index("c")
        rows = x.shape[0] // 2
        self.sent = lax.dynamic_slice_in_dim(x, (1 - c) * rows, rows, 0).astype(BF16)
        self.kept = lax.dynamic_slice_in_dim(x, c * rows, rows, 0)

    def cores(self):
        l = lax.axis_index("l")
        half = self.kept.astype(F32) + swap(self.sent, "c").astype(F32)
        rows = half.shape[0] // 2
        self.sent = lax.dynamic_slice_in_dim(half, (1 - l) * rows, rows, 0).astype(BF16)
        self.kept = lax.dynamic_slice_in_dim(half, l * rows, rows, 0)

    def chips(self):
        return self.kept + swap(self.sent, "l").astype(F32)


def shuffle(plane, v, back=False):
    if len(plane) == 1:
        return v
    share = v.shape[-1] // 4
    b = [v[..., i * share : (i + 1) * share] for i in range(4)]
    if back:
        b = [b[0], b[1], b[3], b[2]]
    x, y = lax.axis_index("x"), lax.axis_index("y")
    b = [jnp.where(x == 0, b[i], b[i ^ 1]) for i in range(4)]
    b = [jnp.where(y == 0, b[i], b[i ^ 2]) for i in range(4)]
    if not back:
        b = [b[0], b[1], b[3], b[2]]
    return cat(b, -1)


class PlaneGather:
    def __init__(self, plane, piece, first):
        if len(plane) == 1:
            self.parts = [lax.all_gather(piece, plane, axis=0, tiled=True)]
            self.near, self.far = self.parts, self.parts[0]
            return
        near = {axis: swap(piece, axis) for axis in plane}
        second = "y" if first == "x" else "x"
        self.far = swap(near[first], second)
        self.near = [near["x"], near["y"]]
        self.parts = [piece, near["x"], self.far, near["y"]]

    def whole(self):
        return by_rows(cat(self.parts) if len(self.parts) > 1 else self.parts[0])


class PlaneSum:
    def __init__(self, plane, pairs, first):
        self.plane, self.pairs, self.first = plane, pairs, first
        width = pairs[0][0].shape[1]
        self.w = w = width // 4
        if len(plane) == 1:
            self.sent = self.product(0, width)
        elif first == "x":
            self.sent = self.product(w, 3 * w)
        else:
            self.sent = self.product(2 * w, 4 * w)

    def product(self, start, stop):
        parts = [dot(left[:, start:stop], right, 0, 0).astype(BF16) for left, right in self.pairs]
        return cat(parts, 1) if len(parts) > 1 else parts[0]

    def second(self, ties=()):
        if len(self.plane) == 1:
            self.total = lax.psum_scatter(self.sent, self.plane, scatter_dimension=0, tiled=True).astype(F32)
            self.sent = self.got = self.total
            return
        w = self.w
        self.got = got = after(swap(self.sent, self.first), *ties)
        if self.first == "x":
            self.axis, mine, other, other_at = "y", got[:w], got[w:], 3
        else:
            self.axis, mine, other, other_at = "x", got[w:], got[:w], 1
        other = self.product(other_at * w, (other_at + 1) * w).astype(F32) + other.astype(F32)
        self.sent = other.astype(BF16)
        self.total = self.product(0, w).astype(F32) + mine.astype(F32)

    def last(self):
        if len(self.plane) > 1:
            self.total = self.total + swap(self.sent, self.axis).astype(F32)


class GroupSum:
    def __init__(self, plane, sources):
        self.columns = [right.shape[1] for _, right, _ in sources]
        self.here = PlaneSum(plane, [(left, right) for left, right, _ in sources], "x")
        self.there = PlaneSum(plane, [(left, right) for left, _, right in sources], "y")
        self.sent = [self.here.sent, self.there.sent]

    def second(self, ties=()):
        self.here.second(ties)
        self.there.second(ties)
        self.sent = [self.here.sent, self.there.sent]

    def line(self):
        self.there.last()
        self.sent = [self.there.total.astype(BF16)]
        self.here.last()
        self.sent.append(self.here.total)

    def cores(self, ties=()):
        got = swap(self.sent[0], "h")
        mine = self.here.total + (after(got, *ties) if ties else got).astype(F32)
        c = lax.axis_index("c")
        rows = mine.shape[0] // 2
        self.given = lax.dynamic_slice_in_dim(mine, (1 - c) * rows, rows, 0).astype(BF16)
        self.kept = lax.dynamic_slice_in_dim(mine, c * rows, rows, 0)

    def results(self):
        c = lax.axis_index("c")
        got = swap(self.given, "c").astype(F32)
        results, start = [], 0
        for n in self.columns:
            results.append(by_index(c, self.kept[:, start : start + n], got[:, start : start + n], 1))
            start += n
        return results


def pack(groups, common=()):
    c = lax.axis_index("c")
    mine, other, results, start = [], [], [], 0
    for shards in groups:
        columns = sum(s.shape[1] // 2 for s in shards) + sum(s.shape[1] for s in common)
        filled = list(common)
        if columns % 128:
            filled.append(jnp.zeros((shards[0].shape[0], 128 - columns % 128), BF16))
        low = cat([s[:, : s.shape[1] // 2] for s in shards] + filled, 1)
        high = cat([s[:, s.shape[1] // 2 :] for s in shards] + filled, 1)
        mine.append(jnp.where(c == 0, low, high))
        other.append(jnp.where(c == 0, high, low))
    got = swap(cat(other, 1), "c")
    for block in mine:
        results.append(by_rows(by_index(c, block, got[:, start : start + block.shape[1]])))
        start += block.shape[1]
    return results


def tall(x):
    padding = 128 - x.shape[0]
    wide = cat([x.astype(F32), jnp.zeros((padding, x.shape[1]), F32)])
    return wide.astype(BF16), wide.T.astype(BF16)


def attend_kernel(code_ref, doc_ref, qkv_ref, ctx_ref, lse_ref, bias_ref):
    length = qkv_ref.shape[-1]
    heads = qkv_ref.shape[0] // (3 * HD)
    block = min(256, length)
    fill_bias(code_ref, doc_ref, bias_ref)
    for head in range(heads):
        part = [slice((i * heads + head) * HD, (i * heads + head + 1) * HD) for i in range(3)]
        v = qkv_ref[part[2]]
        q, _ = tall(qkv_ref[part[0]])
        _, k = tall(qkv_ref[part[1]])
        for start in range(0, length, block):
            end = start + block
            cols = slice(start, end)
            s = dot(k[:end], q[:, cols], 1, 0) * SCALE + bias_ref[:end, cols]
            top = jnp.max(s, axis=0, keepdims=True)
            e = jnp.exp(s - top)
            total = jnp.sum(e, axis=0, keepdims=True)
            p = (e * (1.0 / total)).astype(BF16)
            ctx_ref[part[0], cols] = dot(v[:, :end], p, 1, 0).astype(BF16)
            lse_ref[head : head + 1, cols] = top + jnp.log(total)


def sum_kernel(terms, weights, extra, *refs):
    weight_refs, left_refs, out_ref = refs[:weights], refs[weights:-1], refs[-1]
    total = dot(left_refs[-2][...], left_refs[-1][...], 0, 0) if extra else None
    for (which, start, stop, side), left_ref in zip(terms, left_refs):
        right = weight_refs[which][:, start:stop]
        part = dot(left_ref[...], right, side, 1)
        total = part if total is None else total + part
    out_ref[...] = total.astype(BF16)


def sum_dots(weights, terms, extra=()):
    left, side = terms[0][0], terms[0][4]
    rows, width = left.shape[1 - side], weights[0].shape[0]
    tile, wide = min(512, rows), 512
    in_specs = [pl.BlockSpec((wide, w.shape[1]), lambda n, m: (n, 0)) for w in weights]
    for left, _, _, _, side in terms:
        if side == 1:
            in_specs.append(pl.BlockSpec((tile, left.shape[1]), lambda n, m: (m, 0)))
        else:
            in_specs.append(pl.BlockSpec((left.shape[0], tile), lambda n, m: (0, m)))
    if extra:
        in_specs.append(pl.BlockSpec((extra[0].shape[0], tile), lambda n, m: (0, m)))
        in_specs.append(pl.BlockSpec((extra[1].shape[0], wide), lambda n, m: (0, n)))
    return pl.pallas_call(
        functools.partial(sum_kernel, [t[1:] for t in terms], len(weights), len(extra) > 0),
        grid=(width // wide, rows // tile),
        in_specs=in_specs,
        out_specs=pl.BlockSpec((tile, wide), lambda n, m: (m, n)),
        out_shape=jax.ShapeDtypeStruct((rows, width), BF16),
        compiler_params=pltpu.CompilerParams(vmem_limit_bytes=VMEM_LIMIT),
        cost_estimate=pl.CostEstimate(
            flops=2 * rows * width * sum(t[3] - t[2] for t in terms),
            bytes_accessed=2 * sum(w.size for w in weights) + 8 * sum(t[0].size for t in terms),
            transcendentals=0,
        ),
    )(*weights, *[t[0] for t in terms], *extra)


def fill_bias(code_ref, doc_ref, bias_ref):
    length = bias_ref.shape[0]
    block = min(256, length)
    for start in range(0, length, block):
        u = start + lax.broadcasted_iota(jnp.int32, (block, length), 0)
        t = lax.broadcasted_iota(jnp.int32, (block, length), 1)
        same = code_ref[start : start + block, :] == doc_ref[...]
        allow = ((u <= t) & same) | (u == t)
        bias_ref[start : start + block, :] = jnp.where(allow, 0.0, NEG)


def attend_back_kernel(code_ref, doc_ref, qkv_ref, lse_ref, grad_ref, out_ref, bias_ref, acc_ref):
    length = qkv_ref.shape[-1]
    heads = qkv_ref.shape[0] // (3 * HD)
    block = min(256, length)
    fill_bias(code_ref, doc_ref, bias_ref)
    for head in range(heads):
        part = [slice((i * heads + head) * HD, (i * heads + head + 1) * HD) for i in range(3)]
        q, kt, g = qkv_ref[part[0]], qkv_ref[part[1]], grad_ref[part[0]]
        q_wide, _ = tall(q)
        g_wide, _ = tall(g)
        _, k = tall(kt)
        _, v = tall(qkv_ref[part[2]])
        acc_ref[...] = jnp.zeros_like(acc_ref)
        for start in range(0, length, block):
            end = start + block
            cols = slice(start, end)
            s = dot(k[:end], q_wide[:, cols], 1, 0) * SCALE + bias_ref[:end, cols]
            p = jnp.exp(s - lse_ref[head : head + 1, cols])
            dp = dot(v[:end], g_wide[:, cols], 1, 0)
            inner = jnp.sum(p * dp, axis=0, keepdims=True)
            ds = (p * (dp - inner)).astype(BF16)
            out_ref[part[0], cols] = (dot(kt[:, :end], ds, 1, 0) * SCALE).astype(BF16)
            acc_ref[0, :, :end] += dot(q[:, cols], ds, 1, 1)
            acc_ref[1, :, :end] += dot(g[:, cols], p.astype(BF16), 1, 1)
        out_ref[part[1]] = (acc_ref[0] * SCALE).astype(BF16)
        out_ref[part[2]] = acc_ref[1].astype(BF16)


def attend(code, doc, qkv):
    heads, length = qkv.shape[0] // (3 * HD), qkv.shape[1]
    return pl.pallas_call(
        attend_kernel,
        out_shape=[
            jax.ShapeDtypeStruct((heads * HD, length), BF16),
            jax.ShapeDtypeStruct((heads, length), F32),
        ],
        scratch_shapes=[pltpu.VMEM((length, length), F32)],
        compiler_params=pltpu.CompilerParams(vmem_limit_bytes=VMEM_LIMIT),
        cost_estimate=pl.CostEstimate(
            flops=heads * length * length * HD * 4,
            bytes_accessed=heads * HD * length * 8,
            transcendentals=heads * length * length,
        ),
    )(code, doc, qkv)


def attend_back(code, doc, qkv, lse, grad):
    heads, length = qkv.shape[0] // (3 * HD), qkv.shape[1]
    return pl.pallas_call(
        attend_back_kernel,
        out_shape=jax.ShapeDtypeStruct(qkv.shape, BF16),
        scratch_shapes=[pltpu.VMEM((length, length), F32), pltpu.VMEM((2, HD, length), F32)],
        compiler_params=pltpu.CompilerParams(vmem_limit_bytes=VMEM_LIMIT),
        cost_estimate=pl.CostEstimate(
            flops=heads * length * length * HD * 10,
            bytes_accessed=heads * HD * length * 14,
            transcendentals=heads * length * length,
        ),
    )(code, doc, qkv, lse, grad)


def table_kernel(alpha_ref, eta_ref, keep_ref, table_ref, state_ref):
    spans = table_ref.shape[0]
    place = lax.broadcasted_iota(jnp.int32, (1, table_ref.shape[1]), 1)
    state = jnp.zeros((1, table_ref.shape[1]), F32)
    memory = jnp.zeros((1, table_ref.shape[1]), F32)
    for c in range(spans):
        kept = keep_ref[c : c + 1, :]
        table_ref[c : c + 1, :] = memory * kept
        state_ref[c : c + 1, :] = state * kept
        state = eta_ref[c : c + 1, :] * kept * state + jnp.where(place == c, 1.0, 0.0)
        memory = alpha_ref[c : c + 1, :] * kept * memory + state


def table_back_kernel(alpha_ref, eta_ref, keep_ref, table_ref, state_ref, grad_ref, out_ref, ga_ref, ge_ref):
    spans = table_ref.shape[0]
    wide = (1, table_ref.shape[1])
    grad_state = jnp.zeros(wide, F32)
    grad_memory = jnp.zeros(wide, F32)
    for c in reversed(range(spans)):
        kept = keep_ref[c : c + 1, :]
        grad_state = grad_state + grad_memory
        ga_ref[c : c + 1, :] = grad_memory * table_ref[c : c + 1, :]
        ge_ref[c : c + 1, :] = grad_state * state_ref[c : c + 1, :]
        grad_state = eta_ref[c : c + 1, :] * kept * grad_state
        grad_memory = kept * (alpha_ref[c : c + 1, :] * grad_memory + grad_ref[c : c + 1, :])
    out_ref[0] = jnp.broadcast_to(jnp.sum(ga_ref[...], axis=1, keepdims=True), out_ref.shape[1:])
    out_ref[1] = jnp.broadcast_to(jnp.sum(ge_ref[...], axis=1, keepdims=True), out_ref.shape[1:])


def span_table(alpha, eta, keep):
    spans = alpha.shape[0]
    wide = lambda v: jnp.broadcast_to(v[:, None], (spans, 128))
    square = jax.ShapeDtypeStruct((spans, 128), F32)
    args = (wide(alpha), wide(eta), wide(keep))
    table, state = pl.pallas_call(table_kernel, out_shape=[square, square])(*args)
    return table, (args, table, state)


def span_table_back(kept, grad):
    args, table, state = kept
    spans = table.shape[0]
    scratch = pltpu.VMEM((spans, 128), F32)
    grad = jnp.pad(grad, ((0, 0), (0, 128 - grad.shape[1])))
    both = pl.pallas_call(
        table_back_kernel,
        out_shape=jax.ShapeDtypeStruct((2, spans, 128), F32),
        scratch_shapes=[scratch, scratch],
    )(*args, table, state, grad)
    return both[0, :, 0], both[1, :, 0]


def norm_back(values, inverse, gain, grad):
    scaled = grad * gain
    inner = jnp.mean(values * scaled, axis=-1, keepdims=True)
    grad_values = inverse * scaled - values * inverse * inverse * inverse * inner
    grad_gain = jnp.sum(grad * values * inverse, axis=0)
    return grad_values, grad_gain


def inverse_of(values):
    return lax.rsqrt(jnp.mean(values * values, axis=-1, keepdims=True) + EPS)


def all_sum(plane, v):
    for axis in ("l", "h", "c"):
        v = v + swap(v, axis)
    if len(plane) == 1:
        return lax.psum(v, plane)
    for axis in ("x", "y"):
        v = v + swap(v, axis)
    return v


def all_parts(plane, v):
    for axis in ("l", "h", "c"):
        v = by_index(lax.axis_index(axis), v, swap(v, axis))
    if len(plane) == 1:
        return lax.all_gather(v, plane, axis=0, tiled=True)
    for axis in ("x", "y"):
        v = by_index(lax.axis_index(axis), v, swap(v, axis))
    return v


def on_device(
    plane,
    block_in,
    grad_out,
    resets,
    counts,
    gain_in,
    w_forget,
    w_momentum,
    project_in,
    project_out,
    memory_in,
    memory_out,
    gain_mid,
    gate_weight,
    up_weight,
    down_weight,
):
    relative = functools.partial(shuffle, plane)
    absolute = functools.partial(shuffle, plane, back=True)
    c, l = lax.axis_index("c"), lax.axis_index("l")
    quarter, width = block_in.shape
    length = 4 * quarter
    spans = length // CH
    own_spans = quarter // CH
    member = 2 * c + l
    hidden_units = 4 * memory_in.shape[1]
    units, q_cols, ff = memory_in.shape[1] // 2, project_in.shape[2] // 2, gate_weight.shape[1] // 2

    vectors = cat([v[None] for v in (gain_in, w_forget, w_momentum, gain_mid)], 0)
    for axis in ("l", "h"):
        vectors = by_index(lax.axis_index(axis), vectors, swap(vectors, axis), 1)
    first = [memory_in, project_in[0], project_in[1], project_in[2]]
    x_turned = turn(block_in)
    flags = turn(cat([resets, counts[:, None]], 1))
    (share0,) = pack([first], [vectors.T])
    far0 = swap(after(share0, x_turned), "h")
    late = after([memory_out.T, project_out.T, gate_weight, up_weight, down_weight.T], share0)
    share1, share2 = pack([late[:2], late[2:]])
    x_own = relative(x_turned)
    half = by_index(l, x_own, swap(x_own, "l"))
    other_half = swap(half, "c")
    x_full = by_index(c, half, other_half)
    stages = [PlaneGather(plane, share0, "x")]
    share1 = after(share1, *stages[0].near)
    stages.append(PlaneGather(plane, share1, "y"))
    far0 = after(far0, *stages[0].near)
    stages.append(PlaneGather(plane, far0, "x"))
    far1 = swap(after(share1, far0), "h")
    first_here = stages[0].whole()
    both = range(2)
    q_end = units + 3 * q_cols
    out_end = units + q_cols
    vectors = first_here[:, q_end : q_end + 4].T.astype(F32)
    gain_one, gain_two, gates = vectors[0], vectors[3], vectors[1:3]

    x_wide = x_full.astype(F32)
    normed = (x_wide * inverse_of(x_wide) * gain_one).astype(BF16)

    act, slope_pre, qkv, ctx, lse = [], [], [], [], []

    def memory(first):
        pre = dot(normed, first[:, :units], 1, 0)
        sig_pre = jax.nn.sigmoid(pre)
        act.append((pre * sig_pre).astype(BF16))
        slope_pre.append((sig_pre * (1.0 + pre * (1.0 - sig_pre))).astype(BF16))

    memory(first_here)
    far1 = after(far1, *stages[2].near, *stages[1].near, stages[2].far, act[0])
    stages.append(PlaneGather(plane, far1, "y"))
    far2 = swap(after(share2, far1), "h")
    share2 = after(share2, *stages[3].near, stages[1].far, stages[2].far, stages[3].far)
    stages.append(PlaneGather(plane, share2, "x"))
    grad_turned = turn(after(grad_out, far2))
    far2 = after(far2, *stages[4].near, stages[3].far)
    stages.append(PlaneGather(plane, far2, "y"))
    first_layer, second_layer, feed = (
        [first_here, stages[2].whole()],
        [stages[1].whole(), stages[3].whole()],
        [stages[4].whole(), stages[5].whole()],
    )

    resets, count = flags[0, :-1], flags[0, -1]
    positions = jnp.arange(length, dtype=jnp.int32)
    valid = (positions < count).astype(F32)
    keep = (1 - resets).astype(F32)
    doc = jnp.repeat(jnp.cumsum(resets, dtype=jnp.int32), CH).astype(F32)
    code = jnp.where(valid > 0, doc, -1.0)[:, None]
    doc = doc[None, :]

    x_own = x_own.astype(F32)
    inverse_one = inverse_of(x_own)
    span_sums = jnp.sum(normed.reshape(spans, CH, width).astype(F32), axis=1)
    logits = jnp.sum(span_sums[None] * gates[:, None, :], axis=2) / CH
    alpha = jax.nn.sigmoid(logits[0] + ALPHA_SHIFT)
    eta = jax.nn.sigmoid(logits[1] + ETA_SHIFT)
    table, kept_table = span_table(alpha, eta, keep)

    memory(first_layer[1])
    for i in both:
        qkv.append(dot(first_layer[i][:, units:q_end], normed, 0, 1).astype(BF16))
    sim_sum = RowSum((dot(act[0], act[0], 1, 1) + dot(act[1], act[1], 1, 1)) / hidden_units)
    sim_sum.cores()
    sim = sim_sum.chips()
    qkv[1] = after(qkv[1], *stages[4].near)
    for i in both:
        context, logsum = attend(code, doc, qkv[i])
        ctx.append(context)
        lse.append(logsum)
    out_sum = RowSum(
        sum_dots(
            second_layer,
            [(act[i], i, 0, units, 1) for i in both] + [(ctx[i], i, units, out_end, 0) for i in both],
        )
    )
    out_sum.cores()
    out_own = out_sum.chips()
    table_own = lax.dynamic_slice_in_dim(table[:, :spans], member * own_spans, own_spans, 0)
    spread = jnp.repeat(jnp.repeat(table_own, CH, axis=0), CH, axis=1)
    sim = after(sim, *stages[5].near)
    mixing = (sim * spread * valid[None, :] / CH).astype(BF16)
    middle = x_own + out_own + dot(mixing, normed, 1, 0)
    inverse_two = inverse_of(middle)
    mid = (middle * inverse_two * gain_two).astype(BF16)
    mid_all = gather_rows(mid)
    grad_own = relative(grad_turned)
    grad_all = gather_rows(grad_own)

    hidden, grad_gate_pre, grad_up_pre = [], [], []
    for i in both:
        gate = dot(mid_all, feed[i][:, :ff], 1, 0)
        up = dot(mid_all, feed[i][:, ff : 2 * ff], 1, 0)
        grad_hidden = dot(grad_all, feed[i][:, 2 * ff :], 1, 0)
        sigma = jax.nn.sigmoid(gate)
        swish = gate * sigma
        hidden.append((swish * up).astype(BF16))
        grad_gate_pre.append((grad_hidden * up * (sigma * (1.0 + gate * (1.0 - sigma)))).astype(BF16))
        grad_up_pre.append((grad_hidden * swish).astype(BF16))
    mid_sum = RowSum(
        sum_dots(
            feed,
            [(grad_gate_pre[i], i, 0, ff, 1) for i in both] + [(grad_up_pre[i], i, ff, 2 * ff, 1) for i in both],
        )
    )
    mid_sum.cores()
    mid_late, grad_late = after([mid_all, grad_all], mid_sum.sent)
    feed_sum = GroupSum(
        plane, [(mid_late, *grad_gate_pre), (mid_late, *grad_up_pre), (grad_late, *hidden)]
    )
    hidden = after(hidden, mid_sum.sent, *feed_sum.sent)
    ffn_sum = RowSum(sum_dots(feed, [(hidden[i], i, 2 * ff, 3 * ff, 1) for i in both]))
    grad_mid = after(mid_sum.chips(), ffn_sum.sent)

    back_two, grad_gain_two = norm_back(middle, inverse_two, gain_two, grad_mid)
    grad_middle = grad_own.astype(F32) + back_two
    branch = grad_middle.astype(BF16)
    branch_all = gather_rows(branch)
    scaled = dot(branch, normed, 1, 1) / CH * valid[None, :]
    grad_sim_own = (scaled * spread).astype(BF16)
    grad_sim = gather_rows(grad_sim_own)
    grad_blocks = jnp.sum((scaled * sim).reshape(own_spans, CH, spans, CH), axis=(1, 3))
    grad_table = lax.dynamic_update_slice_in_dim(
        jnp.zeros((spans, spans), F32), grad_blocks, member * own_spans, 0
    )

    feed_sum.second()
    branch_all = after(branch_all, *feed_sum.sent)
    out_grad_sum = GroupSum(plane, [(branch_all, *act), (branch_all, ctx[0].T, ctx[1].T)])
    ffn_sum.sent = after(ffn_sum.sent, branch_all)
    ffn_sum.cores()
    branch_all = after(branch_all, *out_grad_sum.sent, ffn_sum.sent)
    grad_pre, grad_qkv = [], []
    for i in both:
        grad_ctx = dot(second_layer[i][:, units:out_end], branch_all, 0, 1).astype(BF16)
        grad_qkv.append(attend_back(code, doc, qkv[i], lse[i], grad_ctx))
    feed_sum.line()
    out_grad_sum.second(grad_qkv)
    normed_late = after(normed, *feed_sum.sent, *grad_qkv, *out_grad_sum.sent)
    qkv_sum = GroupSum(plane, [(normed_late, grad_qkv[0].T, grad_qkv[1].T)])
    out_grad_sum.line()
    grad_sim, branch_late = after([grad_sim, branch_all], *qkv_sum.sent, *out_grad_sum.sent)
    symmetric = (grad_sim.astype(F32) + grad_sim.T.astype(F32)).astype(BF16)
    for i in both:
        grad_act = (
            dot(branch_late, second_layer[i][:, :units], 1, 0) + dot(symmetric, act[i], 1, 0) / hidden_units
        )
        grad_pre.append((grad_act * slope_pre[i].astype(F32)).astype(BF16))
        if i == 0:
            qkv_sum.second()
            feed_sum.cores([grad_pre[0]])
            symmetric, branch_late = after([symmetric, branch_late], grad_pre[0], *qkv_sum.sent, feed_sum.given)
    memory_sum = GroupSum(plane, [(normed, *grad_pre)])
    ffn_sum.sent = after(ffn_sum.sent, *memory_sum.sent)
    block_out = turn(absolute((middle + ffn_sum.chips()).astype(BF16)))
    qkv_sum.line()
    out_grad_sum.cores(memory_sum.sent)
    grad_pre_late = after(grad_pre, *memory_sum.sent, *qkv_sum.sent)
    normed_sum = RowSum(
        sum_dots(
            first_layer,
            [(grad_pre_late[i], i, 0, units, 1) for i in both] + [(grad_qkv[i], i, units, q_end, 0) for i in both],
            (mixing, branch),
        )
    )
    normed_sum.cores()
    memory_sum.second([normed_sum.sent, out_grad_sum.given])
    qkv_sum.cores(memory_sum.sent)

    grad_table = after(grad_table, *memory_sum.sent)
    for axis in ("c", "l"):
        grad_table = grad_table + swap(grad_table, axis)
    grad_alpha, grad_eta = span_table_back(kept_table, grad_table)
    grad_logits = jnp.stack([grad_alpha * alpha * (1.0 - alpha), grad_eta * eta * (1.0 - eta)]) / CH
    grad_vectors = jnp.sum(grad_logits[:, :, None] * span_sums[None], axis=1)
    own_logits = lax.dynamic_slice_in_dim(grad_logits, member * own_spans, own_spans, 1)
    grad_spans = jnp.sum(own_logits[:, :, None] * gates[:, None, :], axis=0)
    grad_normed = after(normed_sum.chips(), *memory_sum.sent, block_out) + jnp.repeat(grad_spans, CH, axis=0)
    back_one, grad_gain_one = norm_back(x_own, inverse_one, gain_one, grad_normed)
    grad_block_in = turn(absolute((grad_middle + back_one).astype(BF16))).astype(F32)

    memory_sum.line()
    memory_sum.cores()
    grad_gate, grad_up, grad_down = feed_sum.results()
    (grad_qkv_sum,) = qkv_sum.results()
    grad_memory_out, grad_project_out = out_grad_sum.results()
    (grad_memory_in,) = memory_sum.results()

    gram = 0.0
    for i in both:
        blocks = act[i].reshape(spans, CH, -1)
        gram = gram + jnp.einsum("cth,csh->cts", blocks, blocks, preferred_element_type=F32)
    written = (normed * valid[:, None].astype(BF16)).reshape(spans, CH, width)
    cross = jnp.einsum("ctd,csd->cts", written, written, preferred_element_type=F32)
    piece = jnp.sum(gram * cross, axis=(1, 2))
    piece = after(piece, *memory_sum.sent)
    for axis in ("c", "l"):
        piece = piece + swap(piece, axis)
    surprise = jnp.sqrt(piece / (hidden_units * width * CH))
    weight = jnp.sum(valid.reshape(spans, CH), axis=1)
    numbers = jnp.stack(
        [jnp.sum(weight * surprise), jnp.sum(weight * alpha), jnp.sum(weight * eta), jnp.sum(weight)]
    )
    small = jnp.stack([grad_gain_one, grad_vectors[0] * 0.25, grad_vectors[1] * 0.25, grad_gain_two])
    small = cat([absolute(small), jnp.pad(numbers[None], ((0, 0), (0, width - 4)))], 0)
    small = all_sum(plane, small)
    logged = small[4, :3] / small[4, 3]
    share = gain_in.shape[0]
    index = lax.axis_index(plane + ("c", "h", "l"))
    mine = lax.dynamic_slice_in_dim(small, index * share, share, 1)
    grad_project_in = jnp.stack(
        [
            cat([grad_qkv_sum[:, (3 * j + i) * q_cols : (3 * j + i + 1) * q_cols] for j in both], 1)
            for i in range(3)
        ]
    )
    return (
        block_out,
        grad_block_in,
        mine[0],
        mine[1],
        mine[2],
        grad_project_in,
        grad_project_out.T,
        grad_memory_in,
        grad_memory_out.T,
        mine[3],
        grad_gate,
        grad_up,
        grad_down.T,
        logged,
    )


def solution(mesh):
    chips, line = mesh.shape["dp"] // 2, mesh.shape["mp"]
    if chips == 4:
        plane, sizes = ("y", "x"), (2, 2)
    else:
        plane, sizes = ("p",), (chips,)
    fine = Mesh(mesh.devices.reshape(sizes + (2, line // 2, 2)), plane + ("c", "h", "l"))
    dp, mp = plane + ("c",), ("h", "l")
    every = dp + mp
    placed = (
        P(every, None),
        P(every, None),
        P(dp, None),
        P(dp),
        P(every),
        P(every),
        P(every),
        P(None, dp, mp),
        P(mp, dp),
        P(dp, mp),
        P(mp, dp),
        P(every),
        P(dp, mp),
        P(dp, mp),
        P(mp, dp),
    )
    return jax.shard_map(
        functools.partial(on_device, plane),
        mesh=fine,
        in_specs=placed,
        out_specs=(
            P(every, None),
            P(every, None),
            P(every),
            P(every),
            P(every),
            P(None, dp, mp),
            P(mp, dp),
            P(dp, mp),
            P(mp, dp),
            P(every),
            P(dp, mp),
            P(dp, mp),
            P(mp, dp),
            P(),
        ),
        check_vma=False,
    )
```

```python
import functools

import jax
import jax.numpy as jnp
from jax import lax
from jax.experimental import pallas as pl
from jax.experimental.layout import Layout, with_layout_constraint
from jax.experimental.pallas import tpu as pltpu
from jax.sharding import Mesh
from jax.sharding import PartitionSpec as P

HD = 96
CH = 64
EPS = 1e-06
ALPHA_SHIFT = 1.5
ETA_SHIFT = 0.5
NEG = -1e30
SCALE = HD ** (-0.5)
F32 = jnp.float32
BF16 = jnp.bfloat16
VMEM_LIMIT = 24 * 1024 * 1024

def dot(a, b, ca, cb):
    return lax.dot_general(a, b, (((ca,), (cb,)), ((), ())), preferred_element_type=F32)


def swap(x, axis):
    return lax.ppermute(x, axis, [(0, 1), (1, 0)])


def turn(x):
    return lax.ppermute(x, ("c", "h"), [(0, 0), (1, 2), (2, 1), (3, 3)])


def after(x, *others):
    if isinstance(x, (list, tuple)):
        return list(lax.optimization_barrier((*x, *others))[: len(x)])
    return lax.optimization_barrier((x, *others))[0]


def cat(parts, axis=0):
    return jnp.concatenate(parts, axis=axis)


def by_rows(x):
    return with_layout_constraint(x, Layout(major_to_minor=tuple(range(x.ndim))))


def by_index(index, first, second, axis=0):
    return cat([jnp.where(index == 0, first, second), jnp.where(index == 0, second, first)], axis)


def gather_rows(x):
    c, l = lax.axis_index("c"), lax.axis_index("l")
    half = by_index(l, x, swap(x, "l"))
    return by_index(c, half, swap(half, "c"))


class RowSum:
    def __init__(self, x):
        c = lax.axis_index("c")
        rows = x.shape[0] // 2
        self.sent = lax.dynamic_slice_in_dim(x, (1 - c) * rows, rows, 0).astype(BF16)
        self.kept = lax.dynamic_slice_in_dim(x, c * rows, rows, 0)

    def cores(self):
        l = lax.axis_index("l")
        half = self.kept.astype(F32) + swap(self.sent, "c").astype(F32)
        rows = half.shape[0] // 2
        self.sent = lax.dynamic_slice_in_dim(half, (1 - l) * rows, rows, 0).astype(BF16)
        self.kept = lax.dynamic_slice_in_dim(half, l * rows, rows, 0)

    def chips(self):
        return self.kept + swap(self.sent, "l").astype(F32)


def shuffle(plane, v, back=False):
    if len(plane) == 1:
        return v
    share = v.shape[-1] // 4
    b = [v[..., i * share : (i + 1) * share] for i in range(4)]
    if back:
        b = [b[0], b[1], b[3], b[2]]
    x, y = lax.axis_index("x"), lax.axis_index("y")
    b = [jnp.where(x == 0, b[i], b[i ^ 1]) for i in range(4)]
    b = [jnp.where(y == 0, b[i], b[i ^ 2]) for i in range(4)]
    if not back:
        b = [b[0], b[1], b[3], b[2]]
    return cat(b, -1)


class PlaneGather:
    def __init__(self, plane, piece, first):
        if len(plane) == 1:
            self.parts = [lax.all_gather(piece, plane, axis=0, tiled=True)]
            self.near, self.far = self.parts, self.parts[0]
            return
        near = {axis: swap(piece, axis) for axis in plane}
        second = "y" if first == "x" else "x"
        self.far = swap(near[first], second)
        self.near = [near["x"], near["y"]]
        self.parts = [piece, near["x"], self.far, near["y"]]

    def whole(self):
        return by_rows(cat(self.parts) if len(self.parts) > 1 else self.parts[0])


class PlaneSum:
    def __init__(self, plane, pairs, first):
        self.plane, self.pairs, self.first = plane, pairs, first
        width = pairs[0][0].shape[1]
        self.w = w = width // 4
        if len(plane) == 1:
            self.sent = self.product(0, width)
        elif first == "x":
            self.sent = self.product(w, 3 * w)
        else:
            self.sent = self.product(2 * w, 4 * w)

    def product(self, start, stop):
        parts = [dot(left[:, start:stop], right, 0, 0).astype(BF16) for left, right in self.pairs]
        return cat(parts, 1) if len(parts) > 1 else parts[0]

    def second(self, ties=()):
        if len(self.plane) == 1:
            self.total = lax.psum_scatter(self.sent, self.plane, scatter_dimension=0, tiled=True).astype(F32)
            self.sent = self.got = self.total
            return
        w = self.w
        self.got = got = after(swap(self.sent, self.first), *ties)
        if self.first == "x":
            self.axis, mine, other, other_at = "y", got[:w], got[w:], 3
        else:
            self.axis, mine, other, other_at = "x", got[w:], got[:w], 1
        other = self.product(other_at * w, (other_at + 1) * w).astype(F32) + other.astype(F32)
        self.sent = other.astype(BF16)
        self.total = self.product(0, w).astype(F32) + mine.astype(F32)

    def last(self):
        if len(self.plane) > 1:
            self.total = self.total + swap(self.sent, self.axis).astype(F32)


class GroupSum:
    def __init__(self, plane, sources):
        self.columns = [right.shape[1] for _, right, _ in sources]
        self.here = PlaneSum(plane, [(left, right) for left, right, _ in sources], "x")
        self.there = PlaneSum(plane, [(left, right) for left, _, right in sources], "y")
        self.sent = [self.here.sent, self.there.sent]

    def second(self, ties=()):
        self.here.second(ties)
        self.there.second(ties)
        self.sent = [self.here.sent, self.there.sent]

    def line(self):
        self.there.last()
        self.sent = [self.there.total.astype(BF16)]
        self.here.last()
        self.sent.append(self.here.total)

    def cores(self, ties=()):
        got = swap(self.sent[0], "h")
        mine = self.here.total + (after(got, *ties) if ties else got).astype(F32)
        c = lax.axis_index("c")
        rows = mine.shape[0] // 2
        self.given = lax.dynamic_slice_in_dim(mine, (1 - c) * rows, rows, 0).astype(BF16)
        self.kept = lax.dynamic_slice_in_dim(mine, c * rows, rows, 0)

    def results(self):
        c = lax.axis_index("c")
        got = swap(self.given, "c").astype(F32)
        results, start = [], 0
        for n in self.columns:
            results.append(by_index(c, self.kept[:, start : start + n], got[:, start : start + n], 1))
            start += n
        return results


def pack(groups, common=()):
    c = lax.axis_index("c")
    mine, other, results, start = [], [], [], 0
    for shards in groups:
        columns = sum(s.shape[1] // 2 for s in shards) + sum(s.shape[1] for s in common)
        filled = list(common)
        if columns % 128:
            filled.append(jnp.zeros((shards[0].shape[0], 128 - columns % 128), BF16))
        low = cat([s[:, : s.shape[1] // 2] for s in shards] + filled, 1)
        high = cat([s[:, s.shape[1] // 2 :] for s in shards] + filled, 1)
        mine.append(jnp.where(c == 0, low, high))
        other.append(jnp.where(c == 0, high, low))
    got = swap(cat(other, 1), "c")
    for block in mine:
        results.append(by_rows(by_index(c, block, got[:, start : start + block.shape[1]])))
        start += block.shape[1]
    return results


def tall(x):
    padding = 128 - x.shape[0]
    wide = cat([x.astype(F32), jnp.zeros((padding, x.shape[1]), F32)])
    return wide.astype(BF16), wide.T.astype(BF16)


def attend_kernel(code_ref, doc_ref, qkv_ref, ctx_ref, lse_ref, bias_ref):
    length = qkv_ref.shape[-1]
    heads = qkv_ref.shape[0] // (3 * HD)
    block = min(256, length)
    fill_bias(code_ref, doc_ref, bias_ref)
    for head in range(heads):
        part = [slice((i * heads + head) * HD, (i * heads + head + 1) * HD) for i in range(3)]
        v = qkv_ref[part[2]]
        q, _ = tall(qkv_ref[part[0]])
        _, k = tall(qkv_ref[part[1]])
        for start in range(0, length, block):
            end = start + block
            cols = slice(start, end)
            s = dot(k[:end], q[:, cols], 1, 0) * SCALE + bias_ref[:end, cols]
            top = jnp.max(s, axis=0, keepdims=True)
            e = jnp.exp(s - top)
            total = jnp.sum(e, axis=0, keepdims=True)
            p = (e * (1.0 / total)).astype(BF16)
            ctx_ref[part[0], cols] = dot(v[:, :end], p, 1, 0).astype(BF16)
            lse_ref[head : head + 1, cols] = top + jnp.log(total)


def sum_kernel(terms, weights, extra, *refs):
    weight_refs, left_refs, out_ref = refs[:weights], refs[weights:-1], refs[-1]
    total = dot(left_refs[-2][...], left_refs[-1][...], 0, 0) if extra else None
    for (which, start, stop, side), left_ref in zip(terms, left_refs):
        right = weight_refs[which][:, start:stop]
        part = dot(left_ref[...], right, side, 1)
        total = part if total is None else total + part
    out_ref[...] = total.astype(BF16)


def sum_dots(weights, terms, extra=()):
    left, side = terms[0][0], terms[0][4]
    rows, width = left.shape[1 - side], weights[0].shape[0]
    tile, wide = min(512, rows), 512
    in_specs = [pl.BlockSpec((wide, w.shape[1]), lambda n, m: (n, 0)) for w in weights]
    for left, _, _, _, side in terms:
        if side == 1:
            in_specs.append(pl.BlockSpec((tile, left.shape[1]), lambda n, m: (m, 0)))
        else:
            in_specs.append(pl.BlockSpec((left.shape[0], tile), lambda n, m: (0, m)))
    if extra:
        in_specs.append(pl.BlockSpec((extra[0].shape[0], tile), lambda n, m: (0, m)))
        in_specs.append(pl.BlockSpec((extra[1].shape[0], wide), lambda n, m: (0, n)))
    return pl.pallas_call(
        functools.partial(sum_kernel, [t[1:] for t in terms], len(weights), len(extra) > 0),
        grid=(width // wide, rows // tile),
        in_specs=in_specs,
        out_specs=pl.BlockSpec((tile, wide), lambda n, m: (m, n)),
        out_shape=jax.ShapeDtypeStruct((rows, width), BF16),
        compiler_params=pltpu.CompilerParams(vmem_limit_bytes=VMEM_LIMIT),
        cost_estimate=pl.CostEstimate(
            flops=2 * rows * width * sum(t[3] - t[2] for t in terms),
            bytes_accessed=2 * sum(w.size for w in weights) + 8 * sum(t[0].size for t in terms),
            transcendentals=0,
        ),
    )(*weights, *[t[0] for t in terms], *extra)


def fill_bias(code_ref, doc_ref, bias_ref):
    length = bias_ref.shape[0]
    block = min(256, length)
    for start in range(0, length, block):
        u = start + lax.broadcasted_iota(jnp.int32, (block, length), 0)
        t = lax.broadcasted_iota(jnp.int32, (block, length), 1)
        same = code_ref[start : start + block, :] == doc_ref[...]
        allow = ((u <= t) & same) | (u == t)
        bias_ref[start : start + block, :] = jnp.where(allow, 0.0, NEG)


def attend_back_kernel(code_ref, doc_ref, qkv_ref, lse_ref, grad_ref, out_ref, bias_ref, acc_ref):
    length = qkv_ref.shape[-1]
    heads = qkv_ref.shape[0] // (3 * HD)
    block = min(256, length)
    fill_bias(code_ref, doc_ref, bias_ref)
    for head in range(heads):
        part = [slice((i * heads + head) * HD, (i * heads + head + 1) * HD) for i in range(3)]
        q, kt, g = qkv_ref[part[0]], qkv_ref[part[1]], grad_ref[part[0]]
        q_wide, _ = tall(q)
        g_wide, _ = tall(g)
        _, k = tall(kt)
        _, v = tall(qkv_ref[part[2]])
        acc_ref[...] = jnp.zeros_like(acc_ref)
        for start in range(0, length, block):
            end = start + block
            cols = slice(start, end)
            s = dot(k[:end], q_wide[:, cols], 1, 0) * SCALE + bias_ref[:end, cols]
            p = jnp.exp(s - lse_ref[head : head + 1, cols])
            dp = dot(v[:end], g_wide[:, cols], 1, 0)
            inner = jnp.sum(p * dp, axis=0, keepdims=True)
            ds = (p * (dp - inner)).astype(BF16)
            out_ref[part[0], cols] = (dot(kt[:, :end], ds, 1, 0) * SCALE).astype(BF16)
            acc_ref[0, :, :end] += dot(q[:, cols], ds, 1, 1)
            acc_ref[1, :, :end] += dot(g[:, cols], p.astype(BF16), 1, 1)
        out_ref[part[1]] = (acc_ref[0] * SCALE).astype(BF16)
        out_ref[part[2]] = acc_ref[1].astype(BF16)


def attend(code, doc, qkv):
    heads, length = qkv.shape[0] // (3 * HD), qkv.shape[1]
    return pl.pallas_call(
        attend_kernel,
        out_shape=[
            jax.ShapeDtypeStruct((heads * HD, length), BF16),
            jax.ShapeDtypeStruct((heads, length), F32),
        ],
        scratch_shapes=[pltpu.VMEM((length, length), F32)],
        compiler_params=pltpu.CompilerParams(vmem_limit_bytes=VMEM_LIMIT),
        cost_estimate=pl.CostEstimate(
            flops=heads * length * length * HD * 4,
            bytes_accessed=heads * HD * length * 8,
            transcendentals=heads * length * length,
        ),
    )(code, doc, qkv)


def attend_back(code, doc, qkv, lse, grad):
    heads, length = qkv.shape[0] // (3 * HD), qkv.shape[1]
    return pl.pallas_call(
        attend_back_kernel,
        out_shape=jax.ShapeDtypeStruct(qkv.shape, BF16),
        scratch_shapes=[pltpu.VMEM((length, length), F32), pltpu.VMEM((2, HD, length), F32)],
        compiler_params=pltpu.CompilerParams(vmem_limit_bytes=VMEM_LIMIT),
        cost_estimate=pl.CostEstimate(
            flops=heads * length * length * HD * 10,
            bytes_accessed=heads * HD * length * 14,
            transcendentals=heads * length * length,
        ),
    )(code, doc, qkv, lse, grad)


def table_kernel(alpha_ref, eta_ref, keep_ref, table_ref, state_ref):
    spans = table_ref.shape[0]
    place = lax.broadcasted_iota(jnp.int32, (1, table_ref.shape[1]), 1)
    state = jnp.zeros((1, table_ref.shape[1]), F32)
    memory = jnp.zeros((1, table_ref.shape[1]), F32)
    for c in range(spans):
        kept = keep_ref[c : c + 1, :]
        table_ref[c : c + 1, :] = memory * kept
        state_ref[c : c + 1, :] = state * kept
        state = eta_ref[c : c + 1, :] * kept * state + jnp.where(place == c, 1.0, 0.0)
        memory = alpha_ref[c : c + 1, :] * kept * memory + state


def table_back_kernel(alpha_ref, eta_ref, keep_ref, table_ref, state_ref, grad_ref, out_ref, ga_ref, ge_ref):
    spans = table_ref.shape[0]
    wide = (1, table_ref.shape[1])
    grad_state = jnp.zeros(wide, F32)
    grad_memory = jnp.zeros(wide, F32)
    for c in reversed(range(spans)):
        kept = keep_ref[c : c + 1, :]
        grad_state = grad_state + grad_memory
        ga_ref[c : c + 1, :] = grad_memory * table_ref[c : c + 1, :]
        ge_ref[c : c + 1, :] = grad_state * state_ref[c : c + 1, :]
        grad_state = eta_ref[c : c + 1, :] * kept * grad_state
        grad_memory = kept * (alpha_ref[c : c + 1, :] * grad_memory + grad_ref[c : c + 1, :])
    out_ref[0] = jnp.broadcast_to(jnp.sum(ga_ref[...], axis=1, keepdims=True), out_ref.shape[1:])
    out_ref[1] = jnp.broadcast_to(jnp.sum(ge_ref[...], axis=1, keepdims=True), out_ref.shape[1:])


def span_table(alpha, eta, keep):
    spans = alpha.shape[0]
    wide = lambda v: jnp.broadcast_to(v[:, None], (spans, 128))
    square = jax.ShapeDtypeStruct((spans, 128), F32)
    args = (wide(alpha), wide(eta), wide(keep))
    table, state = pl.pallas_call(table_kernel, out_shape=[square, square])(*args)
    return table, (args, table, state)


def span_table_back(kept, grad):
    args, table, state = kept
    spans = table.shape[0]
    scratch = pltpu.VMEM((spans, 128), F32)
    grad = jnp.pad(grad, ((0, 0), (0, 128 - grad.shape[1])))
    both = pl.pallas_call(
        table_back_kernel,
        out_shape=jax.ShapeDtypeStruct((2, spans, 128), F32),
        scratch_shapes=[scratch, scratch],
    )(*args, table, state, grad)
    return both[0, :, 0], both[1, :, 0]


def norm_back(values, inverse, gain, grad):
    scaled = grad * gain
    inner = jnp.mean(values * scaled, axis=-1, keepdims=True)
    grad_values = inverse * scaled - values * inverse * inverse * inverse * inner
    grad_gain = jnp.sum(grad * values * inverse, axis=0)
    return grad_values, grad_gain


def inverse_of(values):
    return lax.rsqrt(jnp.mean(values * values, axis=-1, keepdims=True) + EPS)


def all_sum(plane, v):
    for axis in ("l", "h", "c"):
        v = v + swap(v, axis)
    if len(plane) == 1:
        return lax.psum(v, plane)
    for axis in ("x", "y"):
        v = v + swap(v, axis)
    return v


def all_parts(plane, v):
    for axis in ("l", "h", "c"):
        v = by_index(lax.axis_index(axis), v, swap(v, axis))
    if len(plane) == 1:
        return lax.all_gather(v, plane, axis=0, tiled=True)
    for axis in ("x", "y"):
        v = by_index(lax.axis_index(axis), v, swap(v, axis))
    return v


def on_device(
    plane,
    block_in,
    grad_out,
    resets,
    counts,
    gain_in,
    w_forget,
    w_momentum,
    project_in,
    project_out,
    memory_in,
    memory_out,
    gain_mid,
    gate_weight,
    up_weight,
    down_weight,
):
    relative = functools.partial(shuffle, plane)
    absolute = functools.partial(shuffle, plane, back=True)
    c, l = lax.axis_index("c"), lax.axis_index("l")
    quarter, width = block_in.shape
    length = 4 * quarter
    spans = length // CH
    own_spans = quarter // CH
    member = 2 * c + l
    hidden_units = 4 * memory_in.shape[1]
    units, q_cols, ff = memory_in.shape[1] // 2, project_in.shape[2] // 2, gate_weight.shape[1] // 2

    vectors = cat([v[None] for v in (gain_in, w_forget, w_momentum, gain_mid)], 0)
    for axis in ("l", "h"):
        vectors = by_index(lax.axis_index(axis), vectors, swap(vectors, axis), 1)
    first = [memory_in, project_in[0], project_in[1], project_in[2]]
    x_turned = turn(block_in)
    flags = turn(cat([resets, counts[:, None]], 1))
    (share0,) = pack([first], [vectors.T])
    far0 = swap(after(share0, x_turned), "h")
    late = after([memory_out.T, project_out.T, gate_weight, up_weight, down_weight.T], share0)
    share1, share2 = pack([late[:2], late[2:]])
    x_own = relative(x_turned)
    half = by_index(l, x_own, swap(x_own, "l"))
    other_half = swap(half, "c")
    x_full = by_index(c, half, other_half)
    stages = [PlaneGather(plane, share0, "x")]
    share1 = after(share1, *stages[0].near)
    stages.append(PlaneGather(plane, share1, "y"))
    far0 = after(far0, *stages[0].near)
    stages.append(PlaneGather(plane, far0, "x"))
    far1 = swap(after(share1, far0), "h")
    first_here = stages[0].whole()
    both = range(2)
    q_end = units + 3 * q_cols
    out_end = units + q_cols
    vectors = first_here[:, q_end : q_end + 4].T.astype(F32)
    gain_one, gain_two, gates = vectors[0], vectors[3], vectors[1:3]

    x_wide = x_full.astype(F32)
    normed = (x_wide * inverse_of(x_wide) * gain_one).astype(BF16)

    act, slope_pre, qkv, ctx, lse = [], [], [], [], []

    def memory(first):
        pre = dot(normed, first[:, :units], 1, 0)
        sig_pre = jax.nn.sigmoid(pre)
        act.append((pre * sig_pre).astype(BF16))
        slope_pre.append((sig_pre * (1.0 + pre * (1.0 - sig_pre))).astype(BF16))

    memory(first_here)
    far1 = after(far1, *stages[2].near, *stages[1].near, stages[2].far, act[0])
    stages.append(PlaneGather(plane, far1, "y"))
    far2 = swap(after(share2, far1), "h")
    share2 = after(share2, *stages[3].near, stages[1].far, stages[2].far, stages[3].far)
    stages.append(PlaneGather(plane, share2, "x"))
    grad_turned = turn(after(grad_out, far2))
    far2 = after(far2, *stages[4].near, stages[3].far)
    stages.append(PlaneGather(plane, far2, "y"))
    first_layer, second_layer, feed = (
        [first_here, stages[2].whole()],
        [stages[1].whole(), stages[3].whole()],
        [stages[4].whole(), stages[5].whole()],
    )

    resets, count = flags[0, :-1], flags[0, -1]
    positions = jnp.arange(length, dtype=jnp.int32)
    valid = (positions < count).astype(F32)
    keep = (1 - resets).astype(F32)
    doc = jnp.repeat(jnp.cumsum(resets, dtype=jnp.int32), CH).astype(F32)
    code = jnp.where(valid > 0, doc, -1.0)[:, None]
    doc = doc[None, :]

    x_own = x_own.astype(F32)
    inverse_one = inverse_of(x_own)
    span_sums = jnp.sum(normed.reshape(spans, CH, width).astype(F32), axis=1)
    logits = jnp.sum(span_sums[None] * gates[:, None, :], axis=2) / CH
    alpha = jax.nn.sigmoid(logits[0] + ALPHA_SHIFT)
    eta = jax.nn.sigmoid(logits[1] + ETA_SHIFT)
    table, kept_table = span_table(alpha, eta, keep)

    memory(first_layer[1])
    for i in both:
        qkv.append(dot(first_layer[i][:, units:q_end], normed, 0, 1).astype(BF16))
    sim_sum = RowSum((dot(act[0], act[0], 1, 1) + dot(act[1], act[1], 1, 1)) / hidden_units)
    sim_sum.cores()
    sim = sim_sum.chips()
    qkv[1] = after(qkv[1], *stages[4].near)
    for i in both:
        context, logsum = attend(code, doc, qkv[i])
        ctx.append(context)
        lse.append(logsum)
    out_sum = RowSum(
        sum_dots(
            second_layer,
            [(act[i], i, 0, units, 1) for i in both] + [(ctx[i], i, units, out_end, 0) for i in both],
        )
    )
    out_sum.cores()
    out_own = out_sum.chips()
    table_own = lax.dynamic_slice_in_dim(table[:, :spans], member * own_spans, own_spans, 0)
    spread = jnp.repeat(jnp.repeat(table_own, CH, axis=0), CH, axis=1)
    sim = after(sim, *stages[5].near)
    mixing = (sim * spread * valid[None, :] / CH).astype(BF16)
    middle = x_own + out_own + dot(mixing, normed, 1, 0)
    inverse_two = inverse_of(middle)
    mid = (middle * inverse_two * gain_two).astype(BF16)
    mid_all = gather_rows(mid)
    grad_own = relative(grad_turned)
    grad_all = gather_rows(grad_own)

    hidden, grad_gate_pre, grad_up_pre = [], [], []
    for i in both:
        gate = dot(mid_all, feed[i][:, :ff], 1, 0)
        up = dot(mid_all, feed[i][:, ff : 2 * ff], 1, 0)
        grad_hidden = dot(grad_all, feed[i][:, 2 * ff :], 1, 0)
        sigma = jax.nn.sigmoid(gate)
        swish = gate * sigma
        hidden.append((swish * up).astype(BF16))
        grad_gate_pre.append((grad_hidden * up * (sigma * (1.0 + gate * (1.0 - sigma)))).astype(BF16))
        grad_up_pre.append((grad_hidden * swish).astype(BF16))
    mid_sum = RowSum(
        sum_dots(
            feed,
            [(grad_gate_pre[i], i, 0, ff, 1) for i in both] + [(grad_up_pre[i], i, ff, 2 * ff, 1) for i in both],
        )
    )
    mid_sum.cores()
    mid_late, grad_late = after([mid_all, grad_all], mid_sum.sent)
    feed_sum = GroupSum(
        plane, [(mid_late, *grad_gate_pre), (mid_late, *grad_up_pre), (grad_late, *hidden)]
    )
    hidden = after(hidden, mid_sum.sent, *feed_sum.sent)
    ffn_sum = RowSum(sum_dots(feed, [(hidden[i], i, 2 * ff, 3 * ff, 1) for i in both]))
    grad_mid = after(mid_sum.chips(), ffn_sum.sent)

    back_two, grad_gain_two = norm_back(middle, inverse_two, gain_two, grad_mid)
    grad_middle = grad_own.astype(F32) + back_two
    branch = grad_middle.astype(BF16)
    branch_all = gather_rows(branch)
    scaled = dot(branch, normed, 1, 1) / CH * valid[None, :]
    grad_sim_own = (scaled * spread).astype(BF16)
    grad_sim = gather_rows(grad_sim_own)
    grad_blocks = jnp.sum((scaled * sim).reshape(own_spans, CH, spans, CH), axis=(1, 3))
    grad_table = lax.dynamic_update_slice_in_dim(
        jnp.zeros((spans, spans), F32), grad_blocks, member * own_spans, 0
    )

    feed_sum.second()
    branch_all = after(branch_all, *feed_sum.sent)
    out_grad_sum = GroupSum(plane, [(branch_all, *act), (branch_all, ctx[0].T, ctx[1].T)])
    ffn_sum.sent = after(ffn_sum.sent, branch_all)
    ffn_sum.cores()
    branch_all = after(branch_all, *out_grad_sum.sent, ffn_sum.sent)
    grad_pre, grad_qkv = [], []
    for i in both:
        grad_ctx = dot(second_layer[i][:, units:out_end], branch_all, 0, 1).astype(BF16)
        grad_qkv.append(attend_back(code, doc, qkv[i], lse[i], grad_ctx))
    feed_sum.line()
    out_grad_sum.second(grad_qkv)
    normed_late = after(normed, *feed_sum.sent, *grad_qkv, *out_grad_sum.sent)
    qkv_sum = GroupSum(plane, [(normed_late, grad_qkv[0].T, grad_qkv[1].T)])
    out_grad_sum.line()
    grad_sim, branch_late = after([grad_sim, branch_all], *qkv_sum.sent, *out_grad_sum.sent)
    symmetric = (grad_sim.astype(F32) + grad_sim.T.astype(F32)).astype(BF16)
    for i in both:
        grad_act = (
            dot(branch_late, second_layer[i][:, :units], 1, 0) + dot(symmetric, act[i], 1, 0) / hidden_units
        )
        grad_pre.append((grad_act * slope_pre[i].astype(F32)).astype(BF16))
        if i == 0:
            qkv_sum.second()
            feed_sum.cores([grad_pre[0]])
            symmetric, branch_late = after([symmetric, branch_late], grad_pre[0], *qkv_sum.sent, feed_sum.given)
    memory_sum = GroupSum(plane, [(normed, *grad_pre)])
    ffn_sum.sent = after(ffn_sum.sent, *memory_sum.sent)
    block_out = turn(absolute((middle + ffn_sum.chips()).astype(BF16)))
    qkv_sum.line()
    out_grad_sum.cores(memory_sum.sent)
    grad_pre_late = after(grad_pre, *memory_sum.sent, *qkv_sum.sent)
    normed_sum = RowSum(
        sum_dots(
            first_layer,
            [(grad_pre_late[i], i, 0, units, 1) for i in both] + [(grad_qkv[i], i, units, q_end, 0) for i in both],
            (mixing, branch),
        )
    )
    normed_sum.cores()
    memory_sum.second([normed_sum.sent, out_grad_sum.given])
    qkv_sum.cores(memory_sum.sent)

    grad_table = after(grad_table, *memory_sum.sent)
    for axis in ("c", "l"):
        grad_table = grad_table + swap(grad_table, axis)
    grad_alpha, grad_eta = span_table_back(kept_table, grad_table)
    grad_logits = jnp.stack([grad_alpha * alpha * (1.0 - alpha), grad_eta * eta * (1.0 - eta)]) / CH
    grad_vectors = jnp.sum(grad_logits[:, :, None] * span_sums[None], axis=1)
    own_logits = lax.dynamic_slice_in_dim(grad_logits, member * own_spans, own_spans, 1)
    grad_spans = jnp.sum(own_logits[:, :, None] * gates[:, None, :], axis=0)
    grad_normed = after(normed_sum.chips(), *memory_sum.sent, block_out) + jnp.repeat(grad_spans, CH, axis=0)
    back_one, grad_gain_one = norm_back(x_own, inverse_one, gain_one, grad_normed)
    grad_block_in = turn(absolute((grad_middle + back_one).astype(BF16))).astype(F32)

    memory_sum.line()
    memory_sum.cores()
    grad_gate, grad_up, grad_down = feed_sum.results()
    (grad_qkv_sum,) = qkv_sum.results()
    grad_memory_out, grad_project_out = out_grad_sum.results()
    (grad_memory_in,) = memory_sum.results()

    gram = 0.0
    for i in both:
        blocks = act[i].reshape(spans, CH, -1)
        gram = gram + jnp.einsum("cth,csh->cts", blocks, blocks, preferred_element_type=F32)
    written = (normed * valid[:, None].astype(BF16)).reshape(spans, CH, width)
    cross = jnp.einsum("ctd,csd->cts", written, written, preferred_element_type=F32)
    piece = jnp.sum(gram * cross, axis=(1, 2))
    piece = after(piece, *memory_sum.sent)
    for axis in ("c", "l"):
        piece = piece + swap(piece, axis)
    surprise = jnp.sqrt(piece / (hidden_units * width * CH))
    weight = jnp.sum(valid.reshape(spans, CH), axis=1)
    numbers = jnp.stack(
        [jnp.sum(weight * surprise), jnp.sum(weight * alpha), jnp.sum(weight * eta), jnp.sum(weight)]
    )
    small = jnp.stack([grad_gain_one, grad_vectors[0] * 0.25, grad_vectors[1] * 0.25, grad_gain_two])
    small = cat([absolute(small), jnp.pad(numbers[None], ((0, 0), (0, width - 4)))], 0)
    small = all_sum(plane, after(small, memory_sum.given))
    logged = small[4, :3] / small[4, 3]
    share = gain_in.shape[0]
    index = lax.axis_index(plane + ("c", "h", "l"))
    mine = lax.dynamic_slice_in_dim(small, index * share, share, 1)
    grad_project_in = jnp.stack(
        [
            cat([grad_qkv_sum[:, (3 * j + i) * q_cols : (3 * j + i + 1) * q_cols] for j in both], 1)
            for i in range(3)
        ]
    )
    return (
        block_out,
        grad_block_in,
        mine[0],
        mine[1],
        mine[2],
        grad_project_in,
        grad_project_out.T,
        grad_memory_in,
        grad_memory_out.T,
        mine[3],
        grad_gate,
        grad_up,
        grad_down.T,
        logged,
    )


def solution(mesh):
    chips, line = mesh.shape["dp"] // 2, mesh.shape["mp"]
    if chips == 4:
        plane, sizes = ("y", "x"), (2, 2)
    else:
        plane, sizes = ("p",), (chips,)
    fine = Mesh(mesh.devices.reshape(sizes + (2, line // 2, 2)), plane + ("c", "h", "l"))
    dp, mp = plane + ("c",), ("h", "l")
    every = dp + mp
    placed = (
        P(every, None),
        P(every, None),
        P(dp, None),
        P(dp),
        P(every),
        P(every),
        P(every),
        P(None, dp, mp),
        P(mp, dp),
        P(dp, mp),
        P(mp, dp),
        P(every),
        P(dp, mp),
        P(dp, mp),
        P(mp, dp),
    )
    return jax.shard_map(
        functools.partial(on_device, plane),
        mesh=fine,
        in_specs=placed,
        out_specs=(
            P(every, None),
            P(every, None),
            P(every),
            P(every),
            P(every),
            P(None, dp, mp),
            P(mp, dp),
            P(dp, mp),
            P(mp, dp),
            P(every),
            P(dp, mp),
            P(dp, mp),
            P(mp, dp),
            P(),
        ),
        check_vma=False,
    )
```
